32 devices in a mesh: grp: 2 (over x), req: 16 (over z, y, core).
Axes of the slice: x: 2, y: 2, z: 4, core: 2. Of those that a mesh axis runs over, the one named last changes fastest.
Arguments:
- queries: bfloat16 [2, 2048, 1024], P('grp', 'req')
- suffix_kv: bfloat16 [2, 2, 2048, 1024], P('grp', None, 'req')
- prefix_kv: bfloat16 [2, 2, 1024, 1024], P('grp', None, 'req'), may hold values from -6 to 6
- lengths: int32 [2, 12], P('grp'), may hold values from 1 to 512, 2048 in all within a row
Outputs:
- attended: bfloat16 [2, 2048, 1024], P('grp', 'req')
The draws below stay inside these ranges and needn't reach their ends.
Inputs may be any that keep to these rules, and one draw needn't show every extreme that they name: Each group's 12 lengths sum to 2048, the longest exactly 512.
All inputs are finite; a program needn't handle non-finite values.
Results may differ from the reference program's by a relative error of at most 0.0075.
Values may be sent and summed in bfloat16 or wider, within the bound.
No kernel may reach another device: no remote copies, remote signals or barrier semaphores. Data moves between devices by JAX's collectives and lax.ppermute only.
A program may use at most 64 MiB of HBM per device.

```python
import math
import jax
import jax.numpy as jnp
import numpy as np
from jax import lax

HEADS = 16
HEAD = 64
WIN = 1024
REQS = 12
GROUPS = 2
SUFFIX = 2048
HD = 1024
MOST = 512


def shared_keys(key):
    inner = jax.random.fold_in(key, 7)
    values = jax.random.normal(inner, (GROUPS, 2, SUFFIX, HD), jnp.float32)
    values = jnp.clip(values, -6.0, 6.0)
    return values


def draw_suffix_kv(key, part):
    return shared_keys(key).astype(jnp.bfloat16)


def draw_queries(key, part):
    inner = jax.random.fold_in(key, 11)
    base = jnp.clip(jax.random.normal(inner, (GROUPS, SUFFIX, HD), jnp.float32), -6.0, 6.0)
    return base.astype(jnp.bfloat16)


def level_of(stream_key, dims, split, low, largest):
    gain, own = 1.0, jax.random.fold_in(stream_key, 6)
    for axis_at, parts in split:
        draws = jnp.exp(jax.random.uniform(jax.random.fold_in(own, axis_at), (parts,), jnp.float32, low / len(split), largest / len(split)))
        gain = gain * jnp.repeat(draws, dims[axis_at] // parts).reshape([-1 if axis == axis_at else 1 for axis in range(len(dims))])
    return gain


def split_up(amount, total, reach, lean):
    weights = [(1 << 20) // math.isqrt(rank ** lean) + 1 for rank in range(2, amount + 1)]
    spare, given = total - reach - (amount - 1), [1] * (amount - 1)
    while spare > 0:
        movable = [i for i in range(amount - 1) if given[i] < reach]
        mass, remaining = sum([weights[i] for i in movable]), spare
        for i in movable:
            addition = min(reach - given[i], max(1, remaining * weights[i] // mass), spare)
            given[i] = given[i] + addition
            spare = spare - addition
    return np.array([reach] + given)


def ragged(own_key, number_of, total, most, slope):
    if number_of == 2:
        one = jax.random.randint(own_key, (), max(1, total - most), min(most, total - 1) + 1)
        return jnp.stack([one, total - one])
    sizes = jnp.asarray(split_up(number_of, total, most, slope), jnp.int32)
    couples = (number_of - 1) // 2
    donor, taker = sizes[1:1 + 2 * couples:2], sizes[2:2 + 2 * couples:2]
    room = jnp.minimum(donor - 1, most - taker)
    moved = jax.random.randint(jax.random.fold_in(own_key, 1), (couples,), 0, 1 << 20) % (room + 1)
    sizes = sizes.at[1:1 + 2 * couples:2].set(donor - moved).at[2:2 + 2 * couples:2].set(taker + moved)
    return sizes[jax.random.permutation(jax.random.fold_in(own_key, 2), number_of)]


def normal_values(own_key, shape, deviation, limit, split=(), kind=jnp.bfloat16):
    values = deviation * jax.random.normal(own_key, shape, jnp.float32)
    if split:
        values = values * level_of(own_key, shape, split, -0.22, 0.18)
    return jnp.clip(values, -limit, limit).astype(kind)


def setup_inputs(seed: int = 0) -> dict:
    streams_of = jax.random.split(jax.random.key(seed), 5)
    return {
        "queries": draw_queries(jax.random.fold_in(streams_of[4], 71), 0),
        "suffix_kv": draw_suffix_kv(jax.random.fold_in(streams_of[4], 71), 0),
        "prefix_kv": normal_values(streams_of[2], (GROUPS, 2, WIN, HD), 1.0, 6.0, ((0, 2), (2, 16))),
        "lengths": jax.vmap(lambda own: ragged(own, REQS, SUFFIX, MOST, 2))(jax.random.split(streams_of[3], GROUPS)).reshape((GROUPS, REQS)).astype(jnp.int32),
    }


def locate(positions, starts, ends):
    inside = (positions[:, None] >= starts[None, :]) & (positions[:, None] < ends[None, :])
    numbers = jnp.arange(1, starts.shape[0] + 1, dtype=jnp.int32)
    request = jnp.sum(jnp.where(inside, numbers[None, :], 0), axis=1).astype(jnp.int32) - 1
    offset = positions - jnp.sum(jnp.where(inside, starts[None, :], 0), axis=1).astype(jnp.int32)
    return request, offset


def reference(queries, suffix_kv, prefix_kv, lengths):
    block_rows = min(512, SUFFIX)
    results = []
    for group in range(GROUPS):
        lens = lengths[group].astype(jnp.int32)
        ends = jnp.cumsum(lens).astype(jnp.int32)
        starts = ends - lens
        padding = jnp.zeros((2, WIN, HD), jnp.bfloat16)
        padded = jnp.concatenate([padding, suffix_kv[group]], axis=1)
        prefix_keys = prefix_kv[group, 0].astype(jnp.float32).reshape(WIN, HEADS, HEAD)
        prefix_vals = prefix_kv[group, 1].astype(jnp.float32).reshape(WIN, HEADS, HEAD)
        group_queries = queries[group]

        def one_block(number):
            first = (number * block_rows).astype(jnp.int32)
            query = lax.dynamic_slice_in_dim(group_queries, first, block_rows, 0)
            query = query.astype(jnp.float32).reshape(block_rows, HEADS, HEAD)
            near = lax.dynamic_slice_in_dim(padded, first, WIN + block_rows, 1)
            key_index = first - WIN + jnp.arange(WIN + block_rows, dtype=jnp.int32)
            query_index = first + jnp.arange(block_rows, dtype=jnp.int32)
            key_req, key_off = locate(key_index, starts, ends)
            query_req, query_off = locate(query_index, starts, ends)
            near_mask = (key_req[None, :] == query_req[:, None]) & (key_off[None, :] <= query_off[:, None])
            near_mask = near_mask & (query_off[:, None] - key_off[None, :] < WIN) & (key_index[None, :] >= 0)
            prefix_mask = jnp.arange(WIN, dtype=jnp.int32)[None, :] > query_off[:, None]
            mask = jnp.concatenate([prefix_mask, near_mask], axis=1)
            keys = jnp.concatenate([prefix_keys, near[0].astype(jnp.float32).reshape(-1, HEADS, HEAD)], axis=0)
            vals = jnp.concatenate([prefix_vals, near[1].astype(jnp.float32).reshape(-1, HEADS, HEAD)], axis=0)
            score = jnp.einsum("qhd,khd->hqk", query, keys) * 0.125
            score = jnp.where(mask[None], score, -1e30)
            top = jnp.max(score, axis=-1, keepdims=True)
            weight = jnp.where(mask[None], jnp.exp(score - top), 0.0)
            total = jnp.sum(weight, axis=-1)
            rounded = weight.astype(jnp.bfloat16).astype(jnp.float32)
            summed = jnp.einsum("hqk,khd->hqd", rounded, vals) / total[..., None]
            return jnp.transpose(summed, (1, 0, 2)).reshape(block_rows, HD).astype(jnp.bfloat16)

        attended = lax.map(one_block, jnp.arange(SUFFIX // block_rows, dtype=jnp.int32)).reshape(SUFFIX, HD)
        results.append(attended)
    return jnp.stack(results, axis=0)
```

```python
import functools
import math

import jax
import jax.numpy as jnp
from jax import lax
from jax.experimental import pallas as pl
from jax.experimental.pallas import tpu as pltpu
from jax.sharding import PartitionSpec as P

HEADS = 16
HEAD = 64
WIN = 1024
SUB = 4
MINE = HEADS // SUB
WIDE = MINE * HEAD
ROWS = HEAD + 16
SCALE = 0.125 * math.log2(math.e)
LOW = -8e30
NEVER = -3e38

BF16 = jnp.bfloat16
F32 = jnp.float32


def place():
    position = lax.axis_index("req")
    return position // SUB, position % SUB


def partner(sub, distance):
    return jnp.bitwise_xor(sub, distance)


def columns(owner):
    return pl.ds(pl.multiple_of(owner * WIDE, WIDE), WIDE)


def params():
    return pltpu.CompilerParams(vmem_limit_bytes=48 * 1024 * 1024)


def vmem(count):
    return [pl.BlockSpec(memory_space=pltpu.VMEM)] * count


def cost(flops, moved, exps=0):
    return pl.CostEstimate(flops=flops, bytes_accessed=moved, transcendentals=exps)


def cut_kernel(parts, *refs):
    ins, outs = refs[:len(parts)], refs[len(parts):]
    _, sub = place()
    for distance in range(SUB):
        cols = columns(partner(sub, distance))
        at = 0
        for ref, count in zip(ins, parts):
            for part in range(count):
                outs[distance][at] = ref[0, part, :, cols]
                at += 1


def cut(*arrays):
    parts = [a.shape[1] for a in arrays]
    rows = arrays[0].shape[2]
    slab = jax.ShapeDtypeStruct((sum(parts), rows, WIDE), BF16)
    moved = 2 * sum(a.size * 2 for a in arrays)
    return pl.pallas_call(
        functools.partial(cut_kernel, parts),
        out_shape=[slab] * SUB,
        in_specs=vmem(len(arrays)),
        out_specs=vmem(SUB),
        compiler_params=params(),
        cost_estimate=cost(0, moved),
        name="cut",
    )(*arrays)


def exchange(slabs):
    count = lax.axis_size("req")
    got = [slabs[0]]
    for distance in range(1, SUB):
        route = [(i, i ^ distance) for i in range(count)]
        got.append(lax.ppermute(slabs[distance], "req", route))
    return got


def shift(block, blocks):
    count = lax.axis_size("req")
    route = [(i, i + SUB * blocks) for i in range(count) if 0 <= i + SUB * blocks < count]
    return lax.ppermute(block, "req", route)


def lay_kernel(*refs):
    ins, out = refs[:-1], refs[-1]
    _, sub = place()
    rows = ins[0].shape[1]
    for distance, ref in enumerate(ins):
        at = pl.ds(pl.multiple_of(partner(sub, distance) * rows, rows), rows)
        for part in range(ref.shape[0]):
            out[part, at, :] = ref[part]


def lay(slabs):
    parts, rows, width = slabs[0].shape
    return pl.pallas_call(
        lay_kernel,
        out_shape=jax.ShapeDtypeStruct((parts, rows * SUB, width), BF16),
        in_specs=vmem(SUB),
        out_specs=vmem(1)[0],
        compiler_params=params(),
        cost_estimate=cost(0, 4 * SUB * parts * rows * width),
        name="lay",
    )(*slabs)


def request_rows(lens, tokens):
    start = jnp.int32(0)
    found = jnp.zeros_like(tokens)
    for r in range(lens.shape[1]):
        found = jnp.where(tokens >= start, start, found)
        start = start + lens[0, r]
    return found


def request_start(lens, token):
    start = jnp.int32(0)
    found = jnp.int32(0)
    for r in range(lens.shape[1]):
        found = jnp.where(token >= start, start, found)
        start = start + lens[0, r]
    return found


def q_tile(tokens):
    return min(tokens, 256)


def absorb(qm, top, acc, keys, vals, first_key, lo, span, tile, at):
    count = keys.shape[0]
    cols = slice(at, at + tile)
    number = first_key + lax.broadcasted_iota(jnp.int32, (count, tile), 0)
    gap = number - lo
    allowed = (gap >= 0) & (gap <= span)
    turned = jnp.transpose(vals)
    ones = jnp.ones((ROWS - HEAD, count), BF16)
    for h in range(MINE):
        pair = slice(128 * (h // 2), 128 * (h // 2) + 128)
        score = jnp.dot(keys[:, pair], qm[h, :, cols], preferred_element_type=F32)
        score = jnp.where(allowed, score, NEVER)
        old = top[h:h + 1, cols]
        new = jnp.maximum(old, jnp.max(score, axis=0, keepdims=True))
        weight = jnp.exp2((score - new) * SCALE).astype(BF16)
        factor = jnp.exp2((old - new) * SCALE)
        value = jnp.concatenate([turned[h * HEAD:(h + 1) * HEAD], ones], axis=0)
        added = jnp.dot(value, weight, preferred_element_type=F32)
        acc[h, :, cols] = acc[h, :, cols] * factor + added
        top[h:h + 1, cols] = new


def over_suffix(lens, qm, top, acc, keys, vals, first_key, first_query):
    tokens = qm.shape[2]
    tile = q_tile(tokens)
    rows = keys.shape[0]
    piece = min(rows, 256)
    for at in range(0, tokens, tile):
        query = first_query + at
        token = query + lax.broadcasted_iota(jnp.int32, (1, tile), 1)
        lo = jnp.maximum(request_rows(lens, token), token - (WIN - 1))
        least = jnp.maximum(request_start(lens, query), query - (WIN - 1))
        for k in range(0, rows, piece):
            key = first_key + k

            @pl.when((key + piece > least) & (key < query + tile))
            def _():
                absorb(qm, top, acc, keys[k:k + piece], vals[k:k + piece], key, lo, token - lo, tile, at)


def over_prefix(lens, qm, top, acc, keys, vals, first_key, valid, first_query):
    tokens = qm.shape[2]
    tile = q_tile(tokens)
    rows = keys.shape[0]
    for at in range(0, tokens, tile):
        query = first_query + at
        token = query + lax.broadcasted_iota(jnp.int32, (1, tile), 1)
        off = token - request_rows(lens, token)
        start, last = request_start(lens, query), request_start(lens, query + tile - 1)
        least = jnp.where(start == last, query - start, 0)

        @pl.when(valid & (first_key + rows - 1 > least))
        def _():
            absorb(qm, top, acc, keys[...], vals[...], first_key, off + 1, jnp.full_like(off, WIN), tile, at)


def own_kernel(lens, s0, s1, s2, s3, own, qm, top, acc, held):
    block, sub = place()
    rows = s0.shape[1]
    tokens = rows * SUB
    for distance, ref in enumerate((s0, s1, s2, s3)):
        at = pl.ds(pl.multiple_of(partner(sub, distance) * rows, rows), rows)
        for part in range(3):
            held[part, at, :] = ref[part]
    turned = jnp.transpose(held[0])
    for h in range(MINE):
        mine, other = HEAD * (h % 2), HEAD * (1 - h % 2)
        qm[h, mine:mine + HEAD, :] = turned[h * HEAD:(h + 1) * HEAD]
        qm[h, other:other + HEAD, :] = jnp.zeros((HEAD, tokens), BF16)
    top[...] = jnp.full(top.shape, LOW, F32)
    acc[...] = jnp.zeros(acc.shape, F32)
    first = block * tokens
    over_suffix(lens, qm, top, acc, held.at[1], held.at[2], first, first)
    over_prefix(lens, qm, top, acc, own.at[0], own.at[1], block * own.shape[1], True, first)


def begin(lengths, slabs, own):
    rows = slabs[0].shape[1]
    tokens = rows * SUB
    scores = tokens * (tokens + own.shape[1]) * MINE
    return pl.pallas_call(
        own_kernel,
        out_shape=[
            jax.ShapeDtypeStruct((MINE, 2 * HEAD, tokens), BF16),
            jax.ShapeDtypeStruct((8, tokens), F32),
            jax.ShapeDtypeStruct((MINE, ROWS, tokens), F32),
        ],
        in_specs=[pl.BlockSpec(memory_space=pltpu.SMEM)] + vmem(SUB + 1),
        out_specs=vmem(3),
        scratch_shapes=[pltpu.VMEM((3, tokens, WIDE), BF16)],
        compiler_params=params(),
        cost_estimate=cost(4 * HEAD * scores, 4 << 20, scores),
        name="own",
    )(lengths, *slabs, own)


def hop_step(distance, lens, qm, top, acc, left, right):
    block, _ = place()
    blocks = lax.axis_size("req") // SUB
    first = block * qm.shape[2]
    for ref, source in ((left, block - distance), (right, block + distance)):
        valid = (source >= 0) & (source < blocks)
        over_prefix(lens, qm, top, acc, ref.at[0], ref.at[1], source * ref.shape[1], valid, first)


def hop_kernel(distance, lens, qm, top_in, acc_in, left, right, top, acc):
    top[...] = top_in[...]
    acc[...] = acc_in[...]
    hop_step(distance, lens, qm, top, acc, left, right)


def halo_kernel(distance, lens, qm, top_in, acc_in, s0, s1, s2, s3, top, acc, held):
    block, sub = place()
    rows = s0.shape[1]
    for back, ref in enumerate((s0, s1, s2, s3)):
        at = pl.ds(pl.multiple_of(partner(sub, back) * rows, rows), rows)
        for part in range(2):
            held[part, at, :] = ref[part]
    top[...] = top_in[...]
    acc[...] = acc_in[...]
    tokens = qm.shape[2]
    over_suffix(lens, qm, top, acc, held.at[0], held.at[1], (block - distance) * tokens, block * tokens)


def last_kernel(distance, lens, qm, top_in, acc_in, left, right, o0, o1, o2, o3, top, acc):
    _, sub = place()
    top[...] = top_in[...]
    acc[...] = acc_in[...]
    if distance:
        hop_step(distance, lens, qm, top, acc, left, right)
    whole = jnp.concatenate([acc[h, :HEAD] / acc[h, HEAD:HEAD + 1] for h in range(MINE)], axis=0)
    top_rows = jnp.transpose(whole.astype(BF16))
    rows = o0.shape[0]
    for source in range(SUB):
        for back, ref in enumerate((o0, o1, o2, o3)):

            @pl.when(partner(sub, back) == source)
            def _():
                ref[...] = top_rows[source * rows:(source + 1) * rows]


def carry_call(kernel, name, lengths, qm, top, acc, pieces, scratch, keys):
    scores = qm.shape[2] * keys * MINE
    return pl.pallas_call(
        kernel,
        out_shape=[jax.ShapeDtypeStruct(a.shape, a.dtype) for a in (top, acc)],
        in_specs=[pl.BlockSpec(memory_space=pltpu.SMEM)] + vmem(3 + len(pieces)),
        out_specs=vmem(2),
        scratch_shapes=scratch,
        compiler_params=params(),
        cost_estimate=cost(4 * HEAD * scores, 3 << 20, scores),
        name=name,
    )(lengths, qm, top, acc, *pieces)


def finish(distance, lengths, qm, top, acc, left, right):
    tokens = qm.shape[2]
    rows = tokens // SUB
    scores = tokens * left.shape[1] * MINE
    return pl.pallas_call(
        functools.partial(last_kernel, distance),
        out_shape=[jax.ShapeDtypeStruct((rows, WIDE), BF16)] * SUB,
        in_specs=[pl.BlockSpec(memory_space=pltpu.SMEM)] + vmem(5),
        out_specs=vmem(SUB),
        scratch_shapes=[pltpu.VMEM(top.shape, F32), pltpu.VMEM(acc.shape, F32)],
        compiler_params=params(),
        cost_estimate=cost(4 * HEAD * scores, 3 << 20, scores),
        name="last",
    )(lengths, qm, top, acc, left, right)


def join_kernel(s0, s1, s2, s3, out):
    _, sub = place()
    for distance, ref in enumerate((s0, s1, s2, s3)):
        out[0, :, columns(partner(sub, distance))] = ref[...]


def join(slabs):
    rows = slabs[0].shape[0]
    return pl.pallas_call(
        join_kernel,
        out_shape=jax.ShapeDtypeStruct((1, rows, WIDE * SUB), BF16),
        in_specs=vmem(SUB),
        out_specs=vmem(1)[0],
        compiler_params=params(),
        cost_estimate=cost(0, 4 * rows * WIDE * SUB),
        name="join",
    )(*slabs)


def on_device(queries, suffix_kv, prefix_kv, lengths):
    rows = queries.shape[1]
    count = lax.axis_size("req")
    blocks = count // SUB
    tokens = rows * SUB
    longest = count * rows // 4
    reach = -(-(min(WIN, longest) - 1) // tokens)
    reach = min(reach, blocks - 1)

    raw = [shift(suffix_kv, d) for d in range(1, reach + 1)]
    own = lay(exchange(cut(prefix_kv)))
    slabs = exchange(cut(queries[:, None], suffix_kv))
    left = right = own
    hops = []
    for distance in range(1, blocks):
        left, right = shift(left, 1), shift(right, -1)
        hops.append((left, right))
    qm, top, acc = begin(lengths, slabs, own)
    for distance in range(1, reach + 1):
        pieces = exchange(cut(raw[distance - 1]))
        held = pltpu.VMEM((2, tokens, WIDE), BF16)
        top, acc = carry_call(
            functools.partial(halo_kernel, distance), "halo", lengths, qm, top, acc, pieces, [held], tokens
        )
    for distance in range(1, blocks - 1):
        top, acc = carry_call(
            functools.partial(hop_kernel, distance), "hop", lengths, qm, top, acc, hops[distance - 1], [],
            2 * own.shape[1],
        )
    left, right = hops[-1] if hops else (own, own)
    mixed = finish(blocks - 1, lengths, qm, top, acc, left, right)
    return join(exchange(mixed))


def solution(mesh):
    in_specs = (
        P("grp", "req", None),
        P("grp", None, "req", None),
        P("grp", None, "req", None),
        P("grp", None),
    )
    out_specs = P("grp", "req", None)
    return jax.shard_map(
        on_device, mesh=mesh, in_specs=in_specs, out_specs=out_specs, check_vma=False
    )
```

```python
import functools
import math

import jax
import jax.numpy as jnp
from jax import lax
from jax.experimental import pallas as pl
from jax.experimental.pallas import tpu as pltpu
from jax.sharding import PartitionSpec as P

HEADS = 16
HEAD = 64
WIN = 1024
SUB = 4
MINE = HEADS // SUB
WIDE = MINE * HEAD
ROWS = HEAD + 16
SCALE = 0.125 * math.log2(math.e)
LOW = -8e30
NEVER = -3e38

BF16 = jnp.bfloat16
F32 = jnp.float32


def place():
    position = lax.axis_index("req")
    return position // SUB, position % SUB


def partner(sub, distance):
    return jnp.bitwise_xor(sub, distance)


def columns(owner):
    return pl.ds(pl.multiple_of(owner * WIDE, WIDE), WIDE)


def params():
    return pltpu.CompilerParams(vmem_limit_bytes=48 * 1024 * 1024)


def vmem(count):
    return [pl.BlockSpec(memory_space=pltpu.VMEM)] * count


def cost(flops, moved, exps=0):
    return pl.CostEstimate(flops=flops, bytes_accessed=moved, transcendentals=exps)


def cut_kernel(parts, *refs):
    ins, outs = refs[:len(parts)], refs[len(parts):]
    _, sub = place()
    for distance in range(SUB):
        cols = columns(partner(sub, distance))
        at = 0
        for ref, count in zip(ins, parts):
            for part in range(count):
                outs[distance][at] = ref[0, part, :, cols]
                at += 1


def cut(*arrays):
    parts = [a.shape[1] for a in arrays]
    rows = arrays[0].shape[2]
    slab = jax.ShapeDtypeStruct((sum(parts), rows, WIDE), BF16)
    moved = 2 * sum(a.size * 2 for a in arrays)
    return pl.pallas_call(
        functools.partial(cut_kernel, parts),
        out_shape=[slab] * SUB,
        in_specs=vmem(len(arrays)),
        out_specs=vmem(SUB),
        compiler_params=params(),
        cost_estimate=cost(0, moved),
        name="cut",
    )(*arrays)


def exchange(slabs):
    count = lax.axis_size("req")
    got = [slabs[0]]
    for distance in range(1, SUB):
        route = [(i, i ^ distance) for i in range(count)]
        got.append(lax.ppermute(slabs[distance], "req", route))
    return got


def between(block, routes):
    return lax.ppermute(block, "req", [(SUB * a + s, SUB * b + s) for a, b in routes for s in range(SUB)])


def shift(block, blocks, since=0):
    last = lax.axis_size("req") // SUB - 1
    low, high = (since, last - blocks) if blocks > 0 else (-blocks, last - since)
    return between(block, [(b, b + blocks) for b in range(low, high + 1)])


def gather_four(own):
    two = between(own, [(0, 2), (2, 0), (1, 3), (3, 1)])
    one = between(own, [(0, 1), (1, 0), (2, 3), (3, 2)])
    middle = between(own, [(1, 2), (2, 1)])
    ends = between(two, [(2, 3), (1, 0)])
    return [
        (one, lambda b: jnp.bitwise_xor(b, 1)),
        (two, lambda b: jnp.bitwise_xor(b, 2)),
        (middle, lambda b: jnp.where((b == 1) | (b == 2), 3 - b, -1)),
        (ends, lambda b: jnp.where((b == 0) | (b == 3), 3 - b, -1)),
    ]


def gather_row(own, blocks):
    pieces = []
    left = right = own
    for distance in range(1, blocks):
        left, right = shift(left, 1, distance - 1), shift(right, -1, distance - 1)
        pieces.append((left, lambda b, d=distance: b - d))
        pieces.append((right, lambda b, d=distance: b + d))
    return pieces


def lay_kernel(*refs):
    ins, out = refs[:-1], refs[-1]
    _, sub = place()
    rows = ins[0].shape[1]
    for distance, ref in enumerate(ins):
        at = pl.ds(pl.multiple_of(partner(sub, distance) * rows, rows), rows)
        for part in range(ref.shape[0]):
            out[part, at, :] = ref[part]


def lay(slabs):
    parts, rows, width = slabs[0].shape
    return pl.pallas_call(
        lay_kernel,
        out_shape=jax.ShapeDtypeStruct((parts, rows * SUB, width), BF16),
        in_specs=vmem(SUB),
        out_specs=vmem(1)[0],
        compiler_params=params(),
        cost_estimate=cost(0, 4 * SUB * parts * rows * width),
        name="lay",
    )(*slabs)


def request_rows(lens, tokens):
    start = jnp.int32(0)
    found = jnp.zeros_like(tokens)
    for r in range(lens.shape[1]):
        found = jnp.where(tokens >= start, start, found)
        start = start + lens[0, r]
    return found


def request_start(lens, token):
    start = jnp.int32(0)
    found = jnp.int32(0)
    for r in range(lens.shape[1]):
        found = jnp.where(token >= start, start, found)
        start = start + lens[0, r]
    return found


def absorb(qm, top, acc, keys, vals, first_key, lo, span, at, tile):
    count = keys.shape[0]
    cols = slice(at, at + tile)
    heads = range(MINE)
    turned = jnp.transpose(vals)
    ones = jnp.ones((ROWS - HEAD, count), BF16)
    score = [
        jnp.dot(keys[:, 128 * (h // 2):128 * (h // 2) + 128], qm[h, :, cols], preferred_element_type=F32)
        for h in heads
    ]
    number = first_key + lax.broadcasted_iota(jnp.int32, (count, tile), 0)
    allowed = number >= lo
    if span is not None:
        allowed = allowed & (number - lo <= span)
    score = [jnp.where(allowed, s, NEVER) for s in score]
    old = [top[h:h + 1, cols] for h in heads]
    new = [jnp.maximum(o, jnp.max(s, axis=0, keepdims=True)) for o, s in zip(old, score)]
    weight = [jnp.exp2((s - n) * SCALE).astype(BF16) for s, n in zip(score, new)]
    factor = [jnp.exp2((o - n) * SCALE) for o, n in zip(old, new)]
    value = [jnp.concatenate([turned[h * HEAD:(h + 1) * HEAD], ones], axis=0) for h in heads]
    added = [jnp.dot(v, w, preferred_element_type=F32) for v, w in zip(value, weight)]
    held = [acc[h, :, cols] for h in heads]
    for h in heads:
        acc[h, :, cols] = held[h] * factor[h] + added[h]
    for h in heads:
        top[h:h + 1, cols] = new[h]


def over_suffix(lens, qm, top, acc, keys, vals, first_key, first_query, causal):
    tokens = qm.shape[2]
    rows = keys.shape[0]
    piece = min(rows, 256)
    for k in range(0, rows, piece):
        key = first_key + k
        spots = [(k, tokens - k)] if causal else [(at, piece) for at in range(0, tokens, piece)]
        for at, tile in spots:
            query = first_query + at
            least = jnp.maximum(request_start(lens, query), query - (WIN - 1))

            @pl.when(key + piece > least)
            def _():
                token = query + lax.broadcasted_iota(jnp.int32, (1, tile), 1)
                lo = jnp.maximum(request_rows(lens, token), token - (WIN - 1))
                absorb(qm, top, acc, keys[k:k + piece], vals[k:k + piece], key, lo, token - lo, at, tile)


def over_prefix(lens, qm, top, acc, keys, vals, first_key, valid, first_query):
    tokens = qm.shape[2]
    rows = keys.shape[0]
    start, last = request_start(lens, first_query), request_start(lens, first_query + tokens - 1)
    least = jnp.where(start == last, first_query - start, 0)

    @pl.when(valid & (first_key + rows - 1 > least))
    def _():
        token = first_query + lax.broadcasted_iota(jnp.int32, (1, tokens), 1)
        off = token - request_rows(lens, token)
        absorb(qm, top, acc, keys[...], vals[...], first_key, off + 1, None, 0, tokens)


def own_kernel(lens, s0, s1, s2, s3, own, qm, top, acc, held):
    block, sub = place()
    rows = s0.shape[1]
    tokens = rows * SUB
    for distance, ref in enumerate((s0, s1, s2, s3)):
        at = pl.ds(pl.multiple_of(partner(sub, distance) * rows, rows), rows)
        for part in range(3):
            held[part, at, :] = ref[part]
    turned = jnp.transpose(held[0])
    for h in range(MINE):
        mine, other = HEAD * (h % 2), HEAD * (1 - h % 2)
        qm[h, mine:mine + HEAD, :] = turned[h * HEAD:(h + 1) * HEAD]
        qm[h, other:other + HEAD, :] = jnp.zeros((HEAD, tokens), BF16)
    top[...] = jnp.full(top.shape, LOW, F32)
    acc[...] = jnp.zeros(acc.shape, F32)
    first = block * tokens
    over_suffix(lens, qm, top, acc, held.at[1], held.at[2], first, first, True)
    over_prefix(lens, qm, top, acc, own.at[0], own.at[1], block * own.shape[1], True, first)


def begin(lengths, slabs, own):
    rows = slabs[0].shape[1]
    tokens = rows * SUB
    scores = tokens * (tokens + own.shape[1]) * MINE
    return pl.pallas_call(
        own_kernel,
        out_shape=[
            jax.ShapeDtypeStruct((MINE, 2 * HEAD, tokens), BF16),
            jax.ShapeDtypeStruct((8, tokens), F32),
            jax.ShapeDtypeStruct((MINE, ROWS, tokens), F32),
        ],
        in_specs=[pl.BlockSpec(memory_space=pltpu.SMEM)] + vmem(SUB + 1),
        out_specs=vmem(3),
        scratch_shapes=[pltpu.VMEM((3, tokens, WIDE), BF16)],
        compiler_params=params(),
        cost_estimate=cost(4 * HEAD * scores, 4 << 20, scores),
        name="own",
    )(lengths, *slabs, own)


def pieces_step(sources, lens, qm, top, acc, refs):
    block, _ = place()
    blocks = lax.axis_size("req") // SUB
    first = block * qm.shape[2]
    for ref, source in zip(refs, sources):
        number = source(block)
        valid = (number >= 0) & (number < blocks)
        over_prefix(lens, qm, top, acc, ref.at[0], ref.at[1], number * ref.shape[1], valid, first)


def pieces_kernel(sources, lens, qm, top_in, acc_in, *refs):
    *refs, top, acc = refs
    top[...] = top_in[...]
    acc[...] = acc_in[...]
    pieces_step(sources, lens, qm, top, acc, refs)


def halo_kernel(distance, lens, qm, top_in, acc_in, s0, s1, s2, s3, top, acc, held):
    block, sub = place()
    rows = s0.shape[1]
    for back, ref in enumerate((s0, s1, s2, s3)):
        at = pl.ds(pl.multiple_of(partner(sub, back) * rows, rows), rows)
        for part in range(2):
            held[part, at, :] = ref[part]
    top[...] = top_in[...]
    acc[...] = acc_in[...]
    tokens = qm.shape[2]
    over_suffix(lens, qm, top, acc, held.at[0], held.at[1], (block - distance) * tokens, block * tokens, False)


def last_kernel(sources, lens, qm, top_in, acc_in, *refs):
    *refs, o0, o1, o2, o3, top, acc, turned = refs
    _, sub = place()
    top[...] = top_in[...]
    acc[...] = acc_in[...]
    pieces_step(sources, lens, qm, top, acc, refs)
    whole = jnp.concatenate([acc[h, :HEAD] * (1.0 / acc[h, HEAD:HEAD + 1]) for h in range(MINE)], axis=0)
    turned[...] = jnp.transpose(whole.astype(BF16))
    rows = o0.shape[0]
    for back, ref in enumerate((o0, o1, o2, o3)):
        ref[...] = turned[pl.ds(pl.multiple_of(partner(sub, back) * rows, rows), rows)]


def carry_call(kernel, name, lengths, qm, top, acc, pieces, scratch, keys):
    scores = qm.shape[2] * keys * MINE
    return pl.pallas_call(
        kernel,
        out_shape=[jax.ShapeDtypeStruct(a.shape, a.dtype) for a in (top, acc)],
        in_specs=[pl.BlockSpec(memory_space=pltpu.SMEM)] + vmem(3 + len(pieces)),
        out_specs=vmem(2),
        scratch_shapes=scratch,
        compiler_params=params(),
        cost_estimate=cost(4 * HEAD * scores, 3 << 20, scores),
        name=name,
    )(lengths, qm, top, acc, *pieces)


def prefix_call(lengths, qm, top, acc, pieces):
    return carry_call(
        functools.partial(pieces_kernel, [p[1] for p in pieces]), "prefix", lengths, qm, top, acc,
        [p[0] for p in pieces], [], sum(p[0].shape[1] for p in pieces),
    )


def finish(lengths, qm, top, acc, pieces):
    tokens = qm.shape[2]
    rows = tokens // SUB
    scores = tokens * sum(p[0].shape[1] for p in pieces) * MINE
    return pl.pallas_call(
        functools.partial(last_kernel, [p[1] for p in pieces]),
        out_shape=[jax.ShapeDtypeStruct((rows, WIDE), BF16)] * SUB,
        in_specs=[pl.BlockSpec(memory_space=pltpu.SMEM)] + vmem(3 + len(pieces)),
        out_specs=vmem(SUB),
        scratch_shapes=[
            pltpu.VMEM(top.shape, F32),
            pltpu.VMEM(acc.shape, F32),
            pltpu.VMEM((tokens, WIDE), BF16),
        ],
        compiler_params=params(),
        cost_estimate=cost(4 * HEAD * scores, 3 << 20, scores),
        name="last",
    )(lengths, qm, top, acc, *[p[0] for p in pieces])


def join_kernel(s0, s1, s2, s3, out):
    _, sub = place()
    for distance, ref in enumerate((s0, s1, s2, s3)):
        out[0, :, columns(partner(sub, distance))] = ref[...]


def join(slabs):
    rows = slabs[0].shape[0]
    return pl.pallas_call(
        join_kernel,
        out_shape=jax.ShapeDtypeStruct((1, rows, WIDE * SUB), BF16),
        in_specs=vmem(SUB),
        out_specs=vmem(1)[0],
        compiler_params=params(),
        cost_estimate=cost(0, 4 * rows * WIDE * SUB),
        name="join",
    )(*slabs)


def on_device(queries, suffix_kv, prefix_kv, lengths):
    rows = queries.shape[1]
    count = lax.axis_size("req")
    blocks = count // SUB
    tokens = rows * SUB
    longest = count * rows // 4
    reach = -(-(min(WIN, longest) - 1) // tokens)
    reach = min(reach, blocks - 1)

    raw = [shift(suffix_kv, d) for d in range(1, reach + 1)]
    own = lay(exchange(cut(prefix_kv)))
    slabs = exchange(cut(queries[:, None], suffix_kv))
    pieces = gather_four(own) if blocks == 4 else gather_row(own, blocks)
    qm, top, acc = begin(lengths, slabs, own)
    held = pltpu.VMEM((2, tokens, WIDE), BF16)
    early = pieces[:len(pieces) // 2]
    top, acc = prefix_call(lengths, qm, top, acc, early)
    for back in range(1, reach + 1):
        halo = exchange(cut(raw[back - 1]))
        top, acc = carry_call(
            functools.partial(halo_kernel, back), "halo", lengths, qm, top, acc, halo, [held], tokens
        )
    mixed = finish(lengths, qm, top, acc, pieces[len(early):])
    return join(exchange(mixed))


def solution(mesh):
    in_specs = (
        P("grp", "req", None),
        P("grp", None, "req", None),
        P("grp", None, "req", None),
        P("grp", None),
    )
    out_specs = P("grp", "req", None)
    return jax.shard_map(
        on_device, mesh=mesh, in_specs=in_specs, out_specs=out_specs, check_vma=False
    )
```

```python
import functools
import math

import jax
import jax.numpy as jnp
from jax import lax
from jax.experimental import pallas as pl
from jax.experimental.pallas import tpu as pltpu
from jax.sharding import PartitionSpec as P

HEADS = 16
HEAD = 64
WIN = 1024
SUB = 4
MINE = HEADS // SUB
WIDE = MINE * HEAD
ROWS = HEAD + 16
SCALE = 0.125 * math.log2(math.e)
LOW = -8e30
NEVER = -3e38

BF16 = jnp.bfloat16
F32 = jnp.float32


def place():
    position = lax.axis_index("req")
    return position // SUB, position % SUB


def partner(sub, distance):
    return jnp.bitwise_xor(sub, distance)


def columns(owner):
    return pl.ds(pl.multiple_of(owner * WIDE, WIDE), WIDE)


def params():
    return pltpu.CompilerParams(vmem_limit_bytes=48 * 1024 * 1024)


def vmem(count):
    return [pl.BlockSpec(memory_space=pltpu.VMEM)] * count


def cost(flops, moved, exps=0):
    return pl.CostEstimate(flops=flops, bytes_accessed=moved, transcendentals=exps)


def cut_kernel(*refs):
    ins, outs = refs[:-SUB], refs[-SUB:]
    _, sub = place()
    for distance, out in enumerate(outs):
        cols = columns(partner(sub, distance))
        at = 0
        for ref in ins:
            rows = ref.shape[2]
            for part in range(ref.shape[1]):
                out[at:at + rows] = ref[0, part, :, cols]
                at += rows


def cut(*arrays):
    rows = sum(a.shape[1] * a.shape[2] for a in arrays)
    return pl.pallas_call(
        cut_kernel,
        out_shape=[jax.ShapeDtypeStruct((rows, WIDE), BF16)] * SUB,
        in_specs=vmem(len(arrays)),
        out_specs=vmem(SUB),
        compiler_params=params(),
        cost_estimate=cost(0, 4 * SUB * rows * WIDE),
        name="cut",
    )(*arrays)


def exchange(slabs):
    count = lax.axis_size("req")
    got = [slabs[0]]
    for distance in range(1, SUB):
        route = [(i, i ^ distance) for i in range(count)]
        got.append(lax.ppermute(slabs[distance], "req", route))
    return got


def between(block, routes):
    return lax.ppermute(block, "req", [(SUB * a + s, SUB * b + s) for a, b in routes for s in range(SUB)])


def shift(block, blocks, since=0):
    last = lax.axis_size("req") // SUB - 1
    low, high = (since, last - blocks) if blocks > 0 else (-blocks, last - since)
    return between(block, [(b, b + blocks) for b in range(low, high + 1)])


def gather_four(own):
    two = between(own, [(0, 2), (2, 0), (1, 3), (3, 1)])
    one = between(own, [(0, 1), (1, 0), (2, 3), (3, 2)])
    middle = between(own, [(1, 2), (2, 1)])
    return [
        (one, lambda b: jnp.bitwise_xor(b, 1)),
        (middle, lambda b: jnp.where((b == 1) | (b == 2), 3 - b, -1)),
        (two, lambda b: jnp.bitwise_xor(b, 2)),
    ]


def pass_on(two):
    ends = between(two, [(2, 3), (1, 0)])
    return ends, lambda b: jnp.where((b == 0) | (b == 3), 3 - b, -1)


def gather_row(own, blocks):
    pieces = []
    left = right = own
    for distance in range(1, blocks):
        left, right = shift(left, 1, distance - 1), shift(right, -1, distance - 1)
        pieces.append((left, lambda b, d=distance: b - d))
        pieces.append((right, lambda b, d=distance: b + d))
    return pieces


def in_order(slabs, first, rows, out):
    _, sub = place()
    for distance, ref in enumerate(slabs):
        at = pl.ds(pl.multiple_of(partner(sub, distance) * rows, rows), rows)
        out[at, :] = ref[first:first + rows]


def deal_kernel(*refs):
    ins, (own, near, far) = refs[:-3], refs[-3:]
    _, sub = place()
    half = own.shape[0]
    for distance, (out, at) in enumerate(((own, 0), (near, 0), (far, 0), (near, half))):
        cols = columns(partner(sub, distance))
        for ref in ins:
            rows = ref.shape[2]
            for part in range(ref.shape[1]):
                out[at:at + rows] = ref[0, part, :, cols]
                at += rows


def pair_kernel(far, near, out):
    rows = far.shape[0]
    out[:rows] = far[...]
    out[rows:] = near[rows:]


def trade(*arrays):
    rows = sum(a.shape[1] * a.shape[2] for a in arrays)
    slab = jax.ShapeDtypeStruct((rows, WIDE), BF16)
    slabs = jax.ShapeDtypeStruct((2 * rows, WIDE), BF16)
    own, near, far = pl.pallas_call(
        deal_kernel,
        out_shape=[slab, slabs, slab],
        in_specs=vmem(len(arrays)),
        out_specs=vmem(3),
        compiler_params=params(),
        cost_estimate=cost(0, 4 * SUB * rows * WIDE),
        name="deal",
    )(*arrays)
    count = lax.axis_size("req")
    near = lax.ppermute(near, "req", [(i, i ^ 1) for i in range(count)])
    far = pl.pallas_call(
        pair_kernel,
        out_shape=slabs,
        in_specs=vmem(2),
        out_specs=vmem(1)[0],
        compiler_params=params(),
        cost_estimate=cost(0, 8 * rows * WIDE),
        name="pair",
    )(far, near)
    return own, near, lax.ppermute(far, "req", [(i, i ^ 2) for i in range(count)])


def lay_kernel(*refs):
    *slabs, out = refs
    rows = out.shape[1] // SUB
    for part in range(2):
        in_order(slabs, part * rows, rows, out.at[part])


def lay(slabs, rows):
    return pl.pallas_call(
        lay_kernel,
        out_shape=jax.ShapeDtypeStruct((2, rows * SUB, WIDE), BF16),
        in_specs=vmem(SUB),
        out_specs=vmem(1)[0],
        compiler_params=params(),
        cost_estimate=cost(0, 8 * SUB * rows * WIDE),
        name="lay",
    )(*slabs)


def request_rows(lens, tokens):
    start = jnp.int32(0)
    found = jnp.zeros_like(tokens)
    for r in range(lens.shape[1]):
        found = jnp.where(tokens >= start, start, found)
        start = start + lens[0, r]
    return found


def request_start(lens, token):
    start = jnp.int32(0)
    found = jnp.int32(0)
    for r in range(lens.shape[1]):
        found = jnp.where(token >= start, start, found)
        start = start + lens[0, r]
    return found


def absorb(qm, top, acc, keys, vals, first_key, lo, span, at, tile):
    count = keys.shape[0]
    cols = slice(at, at + tile)
    heads = range(MINE)
    turned = jnp.transpose(vals)
    ones = jnp.ones((ROWS - HEAD, count), BF16)
    score = [
        jnp.dot(keys[:, 128 * (h // 2):128 * (h // 2) + 128], qm[h, :, cols], preferred_element_type=F32)
        for h in heads
    ]
    number = first_key + lax.broadcasted_iota(jnp.int32, (count, tile), 0)
    allowed = number >= lo
    if span is not None:
        allowed = allowed & (number - lo <= span)
    score = [jnp.where(allowed, s, NEVER) for s in score]
    old = [top[h:h + 1, cols] for h in heads]
    new = [jnp.maximum(o, jnp.max(s, axis=0, keepdims=True)) for o, s in zip(old, score)]
    weight = [jnp.exp2((s - n) * SCALE).astype(BF16) for s, n in zip(score, new)]
    factor = [jnp.exp2((o - n) * SCALE) for o, n in zip(old, new)]
    value = [jnp.concatenate([turned[h * HEAD:(h + 1) * HEAD], ones], axis=0) for h in heads]
    added = [jnp.dot(v, w, preferred_element_type=F32) for v, w in zip(value, weight)]
    held = [acc[h, :, cols] for h in heads]
    for h in heads:
        acc[h, :, cols] = held[h] * factor[h] + added[h]
    for h in heads:
        top[h:h + 1, cols] = new[h]


def over_suffix(lens, qm, top, acc, keys, vals, first_key, first_query, causal):
    tokens = qm.shape[2]
    rows = keys.shape[0]
    piece = min(rows, 256)
    for k in range(0, rows, piece):
        key = first_key + k
        spots = [(k, tokens - k)] if causal else [(at, piece) for at in range(0, tokens, piece)]
        for at, tile in spots:
            query = first_query + at
            least = jnp.maximum(request_start(lens, query), query - (WIN - 1))

            @pl.when(key + piece > least)
            def _():
                token = query + lax.broadcasted_iota(jnp.int32, (1, tile), 1)
                lo = jnp.maximum(request_rows(lens, token), token - (WIN - 1))
                absorb(qm, top, acc, keys[k:k + piece], vals[k:k + piece], key, lo, token - lo, at, tile)


def over_prefix(lens, qm, top, acc, keys, vals, first_key, valid, first_query):
    tokens = qm.shape[2]
    rows = keys.shape[0]
    start, last = request_start(lens, first_query), request_start(lens, first_query + tokens - 1)
    least = jnp.where(start == last, first_query - start, 0)

    @pl.when(valid & (first_key + rows - 1 > least))
    def _():
        token = first_query + lax.broadcasted_iota(jnp.int32, (1, tokens), 1)
        off = token - request_rows(lens, token)
        absorb(qm, top, acc, keys[...], vals[...], first_key, off + 1, None, 0, tokens)


def begin_kernel(lens, s0, s1, s2, s3, own, qm, top, acc, held):
    block, _ = place()
    tokens = held.shape[0]
    rows = tokens // SUB
    in_order((s0, s1, s2, s3), s0.shape[0] - rows, rows, held)
    turned = jnp.transpose(held[...])
    for h in range(MINE):
        mine, other = HEAD * (h % 2), HEAD * (1 - h % 2)
        qm[h, mine:mine + HEAD, :] = turned[h * HEAD:(h + 1) * HEAD]
        qm[h, other:other + HEAD, :] = jnp.zeros((HEAD, tokens), BF16)
    top[...] = jnp.full(top.shape, LOW, F32)
    acc[...] = jnp.zeros(acc.shape, F32)
    over_prefix(lens, qm, top, acc, own.at[0], own.at[1], block * own.shape[1], True, block * tokens)


def begin(lengths, slabs, own, rows):
    tokens = rows * SUB
    scores = tokens * own.shape[1] * MINE
    return pl.pallas_call(
        begin_kernel,
        out_shape=[
            jax.ShapeDtypeStruct((MINE, 2 * HEAD, tokens), BF16),
            jax.ShapeDtypeStruct((8, tokens), F32),
            jax.ShapeDtypeStruct((MINE, ROWS, tokens), F32),
        ],
        in_specs=[pl.BlockSpec(memory_space=pltpu.SMEM)] + vmem(SUB + 1),
        out_specs=vmem(3),
        scratch_shapes=[pltpu.VMEM((tokens, WIDE), BF16)],
        compiler_params=params(),
        cost_estimate=cost(4 * HEAD * scores, 4 << 20, scores),
        name="begin",
    )(lengths, *slabs, own)


def pieces_step(sources, lens, qm, top, acc, refs):
    block, _ = place()
    blocks = lax.axis_size("req") // SUB
    first = block * qm.shape[2]
    for ref, source in zip(refs, sources):
        number = source(block)
        valid = (number >= 0) & (number < blocks)
        over_prefix(lens, qm, top, acc, ref.at[0], ref.at[1], number * ref.shape[1], valid, first)


def pieces_kernel(sources, lens, qm, top_in, acc_in, *refs):
    *refs, top, acc = refs
    top[...] = top_in[...]
    acc[...] = acc_in[...]
    pieces_step(sources, lens, qm, top, acc, refs)


def suffix_kernel(distances, lens, qm, top_in, acc_in, *refs):
    *slabs, top, acc, held = refs
    block, _ = place()
    tokens = qm.shape[2]
    rows = tokens // SUB
    top[...] = top_in[...]
    acc[...] = acc_in[...]
    if len(slabs) < SUB:
        half = slabs[0].shape[0]
        slabs = [*slabs, slabs[2].at[pl.ds(half, half)]]
    for number, distance in enumerate(distances):
        for part in range(2):
            in_order(slabs, (2 * number + part) * rows, rows, held.at[part])
        first = (block - distance) * tokens
        over_suffix(lens, qm, top, acc, held.at[0], held.at[1], first, block * tokens, distance == 0)


def last_kernel(sources, lens, qm, top_in, acc_in, *refs):
    *refs, o0, o1, o2, o3, top, acc, turned = refs
    _, sub = place()
    top[...] = top_in[...]
    acc[...] = acc_in[...]
    pieces_step(sources, lens, qm, top, acc, refs)
    whole = jnp.concatenate([acc[h, :HEAD] * (1.0 / acc[h, HEAD:HEAD + 1]) for h in range(MINE)], axis=0)
    turned[...] = jnp.transpose(whole.astype(BF16))
    rows = o0.shape[0]
    for back, ref in enumerate((o0, o1, o2, o3)):
        ref[...] = turned[pl.ds(pl.multiple_of(partner(sub, back) * rows, rows), rows)]


def carry_call(kernel, name, lengths, qm, top, acc, pieces, scratch, keys):
    scores = qm.shape[2] * keys * MINE
    return pl.pallas_call(
        kernel,
        out_shape=[jax.ShapeDtypeStruct(a.shape, a.dtype) for a in (top, acc)],
        in_specs=[pl.BlockSpec(memory_space=pltpu.SMEM)] + vmem(3 + len(pieces)),
        out_specs=vmem(2),
        scratch_shapes=scratch,
        compiler_params=params(),
        cost_estimate=cost(4 * HEAD * scores, 3 << 20, scores),
        name=name,
    )(lengths, qm, top, acc, *pieces)


def prefix_call(lengths, qm, top, acc, pieces):
    return carry_call(
        functools.partial(pieces_kernel, [p[1] for p in pieces]), "prefix", lengths, qm, top, acc,
        [p[0] for p in pieces], [], sum(p[0].shape[1] for p in pieces),
    )


def suffix_call(distances, lengths, qm, top, acc, slabs):
    tokens = qm.shape[2]
    return carry_call(
        functools.partial(suffix_kernel, distances), "suffix", lengths, qm, top, acc, slabs,
        [pltpu.VMEM((2, tokens, WIDE), BF16)], tokens * len(distances),
    )


def finish(lengths, qm, top, acc, pieces):
    tokens = qm.shape[2]
    rows = tokens // SUB
    scores = tokens * sum(p[0].shape[1] for p in pieces) * MINE
    return pl.pallas_call(
        functools.partial(last_kernel, [p[1] for p in pieces]),
        out_shape=[jax.ShapeDtypeStruct((rows, WIDE), BF16)] * SUB,
        in_specs=[pl.BlockSpec(memory_space=pltpu.SMEM)] + vmem(3 + len(pieces)),
        out_specs=vmem(SUB),
        scratch_shapes=[
            pltpu.VMEM(top.shape, F32),
            pltpu.VMEM(acc.shape, F32),
            pltpu.VMEM((tokens, WIDE), BF16),
        ],
        compiler_params=params(),
        cost_estimate=cost(4 * HEAD * scores, 3 << 20, scores),
        name="last",
    )(lengths, qm, top, acc, *[p[0] for p in pieces])


def join_kernel(s0, s1, s2, s3, out):
    _, sub = place()
    for distance, ref in enumerate((s0, s1, s2, s3)):
        out[0, :, columns(partner(sub, distance))] = ref[...]


def join(slabs):
    rows = slabs[0].shape[0]
    return pl.pallas_call(
        join_kernel,
        out_shape=jax.ShapeDtypeStruct((1, rows, WIDE * SUB), BF16),
        in_specs=vmem(SUB),
        out_specs=vmem(1)[0],
        compiler_params=params(),
        cost_estimate=cost(0, 4 * rows * WIDE * SUB),
        name="join",
    )(*slabs)


def on_device(queries, suffix_kv, prefix_kv, lengths):
    rows = queries.shape[1]
    count = lax.axis_size("req")
    blocks = count // SUB
    tokens = rows * SUB
    longest = count * rows // 4
    reach = -(-(min(WIN, longest) - 1) // tokens)
    reach = min(reach, blocks - 1)

    raw = [shift(suffix_kv, d) for d in range(1, reach + 1)]
    slabs = exchange(cut(prefix_kv, queries[:, None]))
    near = trade(suffix_kv)
    own = lay(slabs, prefix_kv.shape[2])
    pieces = gather_four(own) if blocks == 4 else gather_row(own, blocks)
    qm, top, acc = begin(lengths, slabs, own, rows)
    top, acc = suffix_call([0], lengths, qm, top, acc, near)
    for back in range(1, reach + 1):
        halo = exchange(cut(raw[back - 1]))
        top, acc = suffix_call([back], lengths, qm, top, acc, halo)
    if blocks == 4:
        two, where = pieces[-1]
        two, top = lax.optimization_barrier((two, top))
        pieces = pieces[:-1] + [(two, where), pass_on(two)]
    top, acc = prefix_call(lengths, qm, top, acc, pieces[:3])
    mixed = finish(lengths, qm, top, acc, pieces[3:])
    return join(exchange(mixed))


def solution(mesh):
    in_specs = (
        P("grp", "req", None),
        P("grp", None, "req", None),
        P("grp", None, "req", None),
        P("grp", None),
    )
    out_specs = P("grp", "req", None)
    return jax.shard_map(
        on_device, mesh=mesh, in_specs=in_specs, out_specs=out_specs, check_vma=False
    )
```

```python
import functools
import math

import jax
import jax.numpy as jnp
from jax import lax
from jax.experimental import pallas as pl
from jax.experimental.pallas import tpu as pltpu
from jax.sharding import PartitionSpec as P

HEADS = 16
HEAD = 64
WIN = 1024
SUB = 4
MINE = HEADS // SUB
WIDE = MINE * HEAD
ROWS = HEAD + 16
SCALE = 0.125 * math.log2(math.e)
LOW = -8e30
NEVER = -3e38

BF16 = jnp.bfloat16
F32 = jnp.float32


def place():
    position = lax.axis_index("req")
    return position // SUB, position % SUB


def partner(sub, distance):
    return jnp.bitwise_xor(sub, distance)


def columns(owner):
    return pl.ds(pl.multiple_of(owner * WIDE, WIDE), WIDE)


def params():
    return pltpu.CompilerParams(vmem_limit_bytes=48 * 1024 * 1024)


def vmem(count):
    return [pl.BlockSpec(memory_space=pltpu.VMEM)] * count


def cost(flops, moved, exps=0):
    return pl.CostEstimate(flops=flops, bytes_accessed=moved, transcendentals=exps)


def cut_kernel(*refs):
    ins, outs = refs[:-SUB], refs[-SUB:]
    _, sub = place()
    for distance, out in enumerate(outs):
        cols = columns(partner(sub, distance))
        at = 0
        for ref in ins:
            rows = ref.shape[2]
            for part in range(ref.shape[1]):
                out[at:at + rows] = ref[0, part, :, cols]
                at += rows


def cut(*arrays):
    rows = sum(a.shape[1] * a.shape[2] for a in arrays)
    return pl.pallas_call(
        cut_kernel,
        out_shape=[jax.ShapeDtypeStruct((rows, WIDE), BF16)] * SUB,
        in_specs=vmem(len(arrays)),
        out_specs=vmem(SUB),
        compiler_params=params(),
        cost_estimate=cost(0, 4 * SUB * rows * WIDE),
        name="cut",
    )(*arrays)


def exchange(slabs):
    count = lax.axis_size("req")
    got = [slabs[0]]
    for distance in range(SUB - 1, 0, -1):
        route = [(i, i ^ distance) for i in range(count)]
        got.insert(1, lax.ppermute(slabs[distance], "req", route))
    return got


def between(block, routes):
    return lax.ppermute(block, "req", [(SUB * a + s, SUB * b + s) for a, b in routes for s in range(SUB)])


def shift(block, blocks, since=0):
    last = lax.axis_size("req") // SUB - 1
    low, high = (since, last - blocks) if blocks > 0 else (-blocks, last - since)
    return between(block, [(b, b + blocks) for b in range(low, high + 1)])


def gather_four(own):
    two = between(own, [(0, 2), (2, 0), (1, 3), (3, 1)])
    one = between(own, [(0, 1), (1, 0), (2, 3), (3, 2)])
    middle = between(own, [(1, 2), (2, 1)])
    return [
        (one, lambda b: jnp.bitwise_xor(b, 1)),
        (middle, lambda b: jnp.where((b == 1) | (b == 2), 3 - b, -1)),
        (two, lambda b: jnp.bitwise_xor(b, 2)),
    ]


def pass_on(two):
    ends = between(two, [(2, 3), (1, 0)])
    return ends, lambda b: jnp.where((b == 0) | (b == 3), 3 - b, -1)


def gather_row(own, blocks):
    pieces = []
    left = right = own
    for distance in range(1, blocks):
        left, right = shift(left, 1, distance - 1), shift(right, -1, distance - 1)
        pieces.append((left, lambda b, d=distance: b - d))
        pieces.append((right, lambda b, d=distance: b + d))
    return pieces


def in_order(slabs, first, rows, out):
    _, sub = place()
    for distance, ref in enumerate(slabs):
        at = pl.ds(pl.multiple_of(partner(sub, distance) * rows, rows), rows)
        out[at, :] = ref[first:first + rows]


def deal_kernel(*refs):
    ins, (own, near, far) = refs[:-3], refs[-3:]
    _, sub = place()
    half = own.shape[0]
    for distance, (out, at) in enumerate(((own, 0), (near, 0), (far, 0), (near, half))):
        cols = columns(partner(sub, distance))
        for ref in ins:
            rows = ref.shape[2]
            for part in range(ref.shape[1]):
                out[at:at + rows] = ref[0, part, :, cols]
                at += rows


def pair_kernel(far, near, out):
    rows = far.shape[0]
    out[:rows] = far[...]
    out[rows:] = near[rows:]


def trade(*arrays, after=None):
    rows = sum(a.shape[1] * a.shape[2] for a in arrays)
    slab = jax.ShapeDtypeStruct((rows, WIDE), BF16)
    slabs = jax.ShapeDtypeStruct((2 * rows, WIDE), BF16)
    own, near, far = pl.pallas_call(
        deal_kernel,
        out_shape=[slab, slabs, slab],
        in_specs=vmem(len(arrays)),
        out_specs=vmem(3),
        compiler_params=params(),
        cost_estimate=cost(0, 4 * SUB * rows * WIDE),
        name="deal",
    )(*arrays)
    count = lax.axis_size("req")
    near = lax.ppermute(near, "req", [(i, i ^ 1) for i in range(count)])
    if after is not None:
        near, _ = lax.optimization_barrier((near, after))
    far = pl.pallas_call(
        pair_kernel,
        out_shape=slabs,
        in_specs=vmem(2),
        out_specs=vmem(1)[0],
        compiler_params=params(),
        cost_estimate=cost(0, 8 * rows * WIDE),
        name="pair",
    )(far, near)
    return own, near, lax.ppermute(far, "req", [(i, i ^ 2) for i in range(count)])


def lay_kernel(*refs):
    *slabs, out = refs
    rows = out.shape[1] // SUB
    for part in range(2):
        in_order(slabs, part * rows, rows, out.at[part])


def lay(slabs, rows):
    return pl.pallas_call(
        lay_kernel,
        out_shape=jax.ShapeDtypeStruct((2, rows * SUB, WIDE), BF16),
        in_specs=vmem(SUB),
        out_specs=vmem(1)[0],
        compiler_params=params(),
        cost_estimate=cost(0, 8 * SUB * rows * WIDE),
        name="lay",
    )(*slabs)


def request_rows(lens, tokens):
    start = jnp.int32(0)
    found = jnp.zeros_like(tokens)
    for r in range(lens.shape[1]):
        found = jnp.where(tokens >= start, start, found)
        start = start + lens[0, r]
    return found


def request_start(lens, token):
    start = jnp.int32(0)
    found = jnp.int32(0)
    for r in range(lens.shape[1]):
        found = jnp.where(token >= start, start, found)
        start = start + lens[0, r]
    return found


def absorb(qm, top, acc, keys, vals, first_key, lo, span, at, tile):
    count = keys.shape[0]
    cols = slice(at, at + tile)
    heads = range(MINE)
    turned = jnp.transpose(vals)
    ones = jnp.ones((ROWS - HEAD, count), BF16)
    score = [
        jnp.dot(keys[:, 128 * (h // 2):128 * (h // 2) + 128], qm[h, :, cols], preferred_element_type=F32)
        for h in heads
    ]
    number = first_key + lax.broadcasted_iota(jnp.int32, (count, tile), 0)
    allowed = number >= lo
    if span is not None:
        allowed = allowed & (number - lo <= span)
    score = [jnp.where(allowed, s, NEVER) for s in score]
    old = [top[h:h + 1, cols] for h in heads]
    new = [jnp.maximum(o, jnp.max(s, axis=0, keepdims=True)) for o, s in zip(old, score)]
    weight = [jnp.exp2((s - n) * SCALE).astype(BF16) for s, n in zip(score, new)]
    factor = [jnp.exp2((o - n) * SCALE) for o, n in zip(old, new)]
    value = [jnp.concatenate([turned[h * HEAD:(h + 1) * HEAD], ones], axis=0) for h in heads]
    added = [jnp.dot(v, w, preferred_element_type=F32) for v, w in zip(value, weight)]
    held = [acc[h, :, cols] for h in heads]
    for h in heads:
        acc[h, :, cols] = held[h] * factor[h] + added[h]
    for h in heads:
        top[h:h + 1, cols] = new[h]


def over_suffix(lens, qm, top, acc, keys, vals, first_key, first_query, causal):
    tokens = qm.shape[2]
    rows = keys.shape[0]
    piece = min(rows, 256)
    for k in range(0, rows, piece):
        key = first_key + k
        spots = [(k, tokens - k)] if causal else [(at, piece) for at in range(0, tokens, piece)]
        for at, tile in spots:
            query = first_query + at
            least = jnp.maximum(request_start(lens, query), query - (WIN - 1))

            @pl.when(key + piece > least)
            def _():
                token = query + lax.broadcasted_iota(jnp.int32, (1, tile), 1)
                lo = jnp.maximum(request_rows(lens, token), token - (WIN - 1))
                absorb(qm, top, acc, keys[k:k + piece], vals[k:k + piece], key, lo, token - lo, at, tile)


def over_prefix(lens, qm, top, acc, keys, vals, first_key, valid, first_query):
    tokens = qm.shape[2]
    rows = keys.shape[0]
    start, last = request_start(lens, first_query), request_start(lens, first_query + tokens - 1)
    least = jnp.where(start == last, first_query - start, 0)

    @pl.when(valid & (first_key + rows - 1 > least))
    def _():
        token = first_query + lax.broadcasted_iota(jnp.int32, (1, tokens), 1)
        off = token - request_rows(lens, token)
        absorb(qm, top, acc, keys[...], vals[...], first_key, off + 1, None, 0, tokens)


def begin_kernel(lens, s0, s1, s2, s3, own, qm, top, acc, held):
    block, _ = place()
    tokens = held.shape[0]
    rows = tokens // SUB
    in_order((s0, s1, s2, s3), s0.shape[0] - rows, rows, held)
    turned = jnp.transpose(held[...])
    for h in range(MINE):
        mine, other = HEAD * (h % 2), HEAD * (1 - h % 2)
        qm[h, mine:mine + HEAD, :] = turned[h * HEAD:(h + 1) * HEAD]
        qm[h, other:other + HEAD, :] = jnp.zeros((HEAD, tokens), BF16)
    top[...] = jnp.full(top.shape, LOW, F32)
    acc[...] = jnp.zeros(acc.shape, F32)
    over_prefix(lens, qm, top, acc, own.at[0], own.at[1], block * own.shape[1], True, block * tokens)


def begin(lengths, slabs, own, rows):
    tokens = rows * SUB
    scores = tokens * own.shape[1] * MINE
    return pl.pallas_call(
        begin_kernel,
        out_shape=[
            jax.ShapeDtypeStruct((MINE, 2 * HEAD, tokens), BF16),
            jax.ShapeDtypeStruct((8, tokens), F32),
            jax.ShapeDtypeStruct((MINE, ROWS, tokens), F32),
        ],
        in_specs=[pl.BlockSpec(memory_space=pltpu.SMEM)] + vmem(SUB + 1),
        out_specs=vmem(3),
        scratch_shapes=[pltpu.VMEM((tokens, WIDE), BF16)],
        compiler_params=params(),
        cost_estimate=cost(4 * HEAD * scores, 4 << 20, scores),
        name="begin",
    )(lengths, *slabs, own)


def pieces_step(sources, lens, qm, top, acc, refs, first):
    block, _ = place()
    blocks = lax.axis_size("req") // SUB
    for ref, source in zip(refs, sources):
        number = source(block)
        valid = (number >= 0) & (number < blocks)
        over_prefix(lens, qm, top, acc, ref.at[0], ref.at[1], number * ref.shape[1], valid, first)


def pieces_kernel(sources, lens, qm, top_in, acc_in, *refs):
    *refs, top, acc = refs
    top[...] = top_in[...]
    acc[...] = acc_in[...]
    block, _ = place()
    pieces_step(sources, lens, qm, top, acc, refs, block * qm.shape[2])


def suffix_kernel(distances, lens, qm, top_in, acc_in, *refs):
    *slabs, top, acc, held = refs
    block, _ = place()
    tokens = qm.shape[2]
    rows = tokens // SUB
    top[...] = top_in[...]
    acc[...] = acc_in[...]
    if len(slabs) < SUB:
        half = slabs[0].shape[0]
        slabs = [*slabs, slabs[2].at[pl.ds(half, half)]]
    for number, distance in enumerate(distances):
        for part in range(2):
            in_order(slabs, (2 * number + part) * rows, rows, held.at[part])
        first = (block - distance) * tokens
        over_suffix(lens, qm, top, acc, held.at[0], held.at[1], first, block * tokens, distance == 0)


def last_kernel(sources, other, lens, qm_in, top_in, acc_in, *refs):
    *refs, straight, cross, qm, top, acc, turned = refs
    block, sub = place()
    half = top.shape[1]
    at = jnp.bitwise_xor(sub // 2, other) * half
    cols = pl.ds(pl.multiple_of(at, half), half)
    qm[...] = qm_in[:, :, cols]
    top[...] = top_in[:, cols]
    acc[...] = acc_in[:, :, cols]
    pieces_step(sources, lens, qm, top, acc, refs, block * 2 * half + at)
    whole = jnp.concatenate([acc[h, :HEAD] * (1.0 / acc[h, HEAD:HEAD + 1]) for h in range(MINE)], axis=0)
    turned[...] = jnp.transpose(whole.astype(BF16))
    rows = straight.shape[0]
    for side, ref in enumerate((straight, cross)):
        ref[...] = turned[pl.ds(pl.multiple_of(jnp.bitwise_xor(sub % 2, side) * rows, rows), rows)]


def carry_call(kernel, name, lengths, qm, top, acc, pieces, scratch, keys):
    scores = qm.shape[2] * keys * MINE
    return pl.pallas_call(
        kernel,
        out_shape=[jax.ShapeDtypeStruct(a.shape, a.dtype) for a in (top, acc)],
        in_specs=[pl.BlockSpec(memory_space=pltpu.SMEM)] + vmem(3 + len(pieces)),
        out_specs=vmem(2),
        scratch_shapes=scratch,
        compiler_params=params(),
        cost_estimate=cost(4 * HEAD * scores, 3 << 20, scores),
        name=name,
    )(lengths, qm, top, acc, *pieces)


def prefix_call(lengths, qm, top, acc, pieces):
    return carry_call(
        functools.partial(pieces_kernel, [p[1] for p in pieces]), "prefix", lengths, qm, top, acc,
        [p[0] for p in pieces], [], sum(p[0].shape[1] for p in pieces),
    )


def suffix_call(distances, lengths, qm, top, acc, slabs):
    tokens = qm.shape[2]
    return carry_call(
        functools.partial(suffix_kernel, distances), "suffix", lengths, qm, top, acc, slabs,
        [pltpu.VMEM((2, tokens, WIDE), BF16)], tokens * len(distances),
    )


def finish(other, lengths, qm, top, acc, pieces):
    half = qm.shape[2] // 2
    rows = half // 2
    scores = half * sum(p[0].shape[1] for p in pieces) * MINE
    return pl.pallas_call(
        functools.partial(last_kernel, [p[1] for p in pieces], other),
        out_shape=[jax.ShapeDtypeStruct((rows, WIDE), BF16)] * 2,
        in_specs=[pl.BlockSpec(memory_space=pltpu.SMEM)] + vmem(3 + len(pieces)),
        out_specs=vmem(2),
        scratch_shapes=[
            pltpu.VMEM((MINE, 2 * HEAD, half), BF16),
            pltpu.VMEM((8, half), F32),
            pltpu.VMEM((MINE, ROWS, half), F32),
            pltpu.VMEM((half, WIDE), BF16),
        ],
        compiler_params=params(),
        cost_estimate=cost(4 * HEAD * scores, 2 << 20, scores),
        name="last",
    )(lengths, qm, top, acc, *[p[0] for p in pieces])


def join_kernel(s0, s1, s2, s3, out):
    _, sub = place()
    for distance, ref in enumerate((s0, s1, s2, s3)):
        out[0, :, columns(partner(sub, distance))] = ref[...]


def join(slabs):
    rows = slabs[0].shape[0]
    return pl.pallas_call(
        join_kernel,
        out_shape=jax.ShapeDtypeStruct((1, rows, WIDE * SUB), BF16),
        in_specs=vmem(SUB),
        out_specs=vmem(1)[0],
        compiler_params=params(),
        cost_estimate=cost(0, 4 * rows * WIDE * SUB),
        name="join",
    )(*slabs)


def on_device(queries, suffix_kv, prefix_kv, lengths):
    rows = queries.shape[1]
    count = lax.axis_size("req")
    blocks = count // SUB
    tokens = rows * SUB
    longest = count * rows // 4
    reach = -(-(min(WIN, longest) - 1) // tokens)
    reach = min(reach, blocks - 1)

    raw = [shift(suffix_kv, d) for d in range(1, reach + 1)]
    slabs = exchange(cut(prefix_kv, queries[:, None]))
    near = trade(suffix_kv, after=slabs[1])
    own = lay(slabs, prefix_kv.shape[2])
    pieces = gather_four(own) if blocks == 4 else gather_row(own, blocks)
    qm, top, acc = begin(lengths, slabs, own, rows)
    top, acc = suffix_call([0], lengths, qm, top, acc, near)
    for back in range(1, reach + 1):
        halo = exchange(cut(raw[back - 1]))
        top, acc = suffix_call([back], lengths, qm, top, acc, halo)
    if blocks == 4:
        two, where = pieces[-1]
        two, top = lax.optimization_barrier((two, top))
        pieces = pieces[:-1] + [(two, where), pass_on(two)]
    top, acc = prefix_call(lengths, qm, top, acc, pieces[:3])
    far = finish(1, lengths, qm, top, acc, pieces[3:])
    near = finish(0, lengths, qm, top, acc, pieces[3:])
    return join(exchange([*near, *far]))


def solution(mesh):
    in_specs = (
        P("grp", "req", None),
        P("grp", None, "req", None),
        P("grp", None, "req", None),
        P("grp", None),
    )
    out_specs = P("grp", "req", None)
    return jax.shard_map(
        on_device, mesh=mesh, in_specs=in_specs, out_specs=out_specs, check_vma=False
    )
```

```python
import functools
import math

import jax
import jax.numpy as jnp
from jax import lax
from jax.experimental import pallas as pl
from jax.experimental.pallas import tpu as pltpu
from jax.sharding import PartitionSpec as P

HEADS = 16
HEAD = 64
WIN = 1024
SUB = 4
MINE = HEADS // SUB
WIDE = MINE * HEAD
ROWS = HEAD + 16
SCALE = 0.125 * math.log2(math.e)
LOW = -8e30
NEVER = -3e38

BF16 = jnp.bfloat16
F32 = jnp.float32


def place():
    position = lax.axis_index("req")
    return position // SUB, position % SUB


def partner(sub, distance):
    return jnp.bitwise_xor(sub, distance)


def columns(owner):
    return pl.ds(pl.multiple_of(owner * WIDE, WIDE), WIDE)


def params():
    return pltpu.CompilerParams(vmem_limit_bytes=48 * 1024 * 1024)


def vmem(count):
    return [pl.BlockSpec(memory_space=pltpu.VMEM)] * count


def cost(flops, moved, exps=0):
    return pl.CostEstimate(flops=flops, bytes_accessed=moved, transcendentals=exps)


def cut_kernel(*refs):
    ins, outs = refs[:-SUB], refs[-SUB:]
    _, sub = place()
    for distance, out in enumerate(outs):
        cols = columns(partner(sub, distance))
        at = 0
        for ref in ins:
            rows = ref.shape[2]
            for part in range(ref.shape[1]):
                out[at:at + rows] = ref[0, part, :, cols]
                at += rows


def cut(*arrays):
    rows = sum(a.shape[1] * a.shape[2] for a in arrays)
    return pl.pallas_call(
        cut_kernel,
        out_shape=[jax.ShapeDtypeStruct((rows, WIDE), BF16)] * SUB,
        in_specs=vmem(len(arrays)),
        out_specs=vmem(SUB),
        compiler_params=params(),
        cost_estimate=cost(0, 4 * SUB * rows * WIDE),
        name="cut",
    )(*arrays)


def exchange(slabs, nearest_after=None):
    count = lax.axis_size("req")
    got = {0: slabs[0]}
    for distance in (2, 3, 1):
        slab = slabs[distance]
        if distance == 1 and nearest_after is not None:
            slab, _ = lax.optimization_barrier((slab, got[nearest_after]))
        got[distance] = lax.ppermute(slab, "req", [(i, i ^ distance) for i in range(count)])
    return [got[distance] for distance in range(SUB)]


def between(block, routes):
    return lax.ppermute(block, "req", [(SUB * a + s, SUB * b + s) for a, b in routes for s in range(SUB)])


def shift(block, blocks, since=0):
    last = lax.axis_size("req") // SUB - 1
    low, high = (since, last - blocks) if blocks > 0 else (-blocks, last - since)
    return between(block, [(b, b + blocks) for b in range(low, high + 1)])


def gather_four(own, top):
    two = between(own, [(0, 2), (2, 0), (1, 3), (3, 1)])
    own, _ = lax.optimization_barrier((own, top))
    one = between(own, [(0, 1), (1, 0), (2, 3), (3, 2)])
    middle = between(own, [(1, 2), (2, 1)])
    return [
        (one, lambda b: jnp.bitwise_xor(b, 1)),
        (middle, lambda b: jnp.where((b == 1) | (b == 2), 3 - b, -1)),
        (two, lambda b: jnp.bitwise_xor(b, 2)),
    ]


def pass_on(two):
    ends = between(two, [(2, 3), (1, 0)])
    return ends, lambda b: jnp.where((b == 0) | (b == 3), 3 - b, -1)


def gather_row(own, blocks):
    pieces = []
    left = right = own
    for distance in range(1, blocks):
        left, right = shift(left, 1, distance - 1), shift(right, -1, distance - 1)
        pieces.append((left, lambda b, d=distance: b - d))
        pieces.append((right, lambda b, d=distance: b + d))
    return pieces


def in_order(slabs, first, rows, out):
    _, sub = place()
    for distance, ref in enumerate(slabs):
        at = pl.ds(pl.multiple_of(partner(sub, distance) * rows, rows), rows)
        out[at, :] = ref[first:first + rows]


def deal_kernel(*refs):
    ins, (own, near, far) = refs[:-3], refs[-3:]
    _, sub = place()
    half = own.shape[0]
    for distance, (out, at) in enumerate(((own, 0), (near, 0), (far, 0), (near, half))):
        cols = columns(partner(sub, distance))
        for ref in ins:
            rows = ref.shape[2]
            for part in range(ref.shape[1]):
                out[at:at + rows] = ref[0, part, :, cols]
                at += rows


def pair_kernel(far, near, out):
    rows = far.shape[0]
    out[:rows] = far[...]
    out[rows:] = near[rows:]


def trade(*arrays, after=None):
    rows = sum(a.shape[1] * a.shape[2] for a in arrays)
    slab = jax.ShapeDtypeStruct((rows, WIDE), BF16)
    slabs = jax.ShapeDtypeStruct((2 * rows, WIDE), BF16)
    own, near, far = pl.pallas_call(
        deal_kernel,
        out_shape=[slab, slabs, slab],
        in_specs=vmem(len(arrays)),
        out_specs=vmem(3),
        compiler_params=params(),
        cost_estimate=cost(0, 4 * SUB * rows * WIDE),
        name="deal",
    )(*arrays)
    count = lax.axis_size("req")
    near = lax.ppermute(near, "req", [(i, i ^ 1) for i in range(count)])
    if after is not None:
        near, _ = lax.optimization_barrier((near, after))
    far = pl.pallas_call(
        pair_kernel,
        out_shape=slabs,
        in_specs=vmem(2),
        out_specs=vmem(1)[0],
        compiler_params=params(),
        cost_estimate=cost(0, 8 * rows * WIDE),
        name="pair",
    )(far, near)
    return own, near, lax.ppermute(far, "req", [(i, i ^ 2) for i in range(count)])


def lay_kernel(*refs):
    *slabs, out = refs
    rows = out.shape[1] // SUB
    for part in range(2):
        in_order(slabs, part * rows, rows, out.at[part])


def lay(slabs, rows):
    return pl.pallas_call(
        lay_kernel,
        out_shape=jax.ShapeDtypeStruct((2, rows * SUB, WIDE), BF16),
        in_specs=vmem(SUB),
        out_specs=vmem(1)[0],
        compiler_params=params(),
        cost_estimate=cost(0, 8 * SUB * rows * WIDE),
        name="lay",
    )(*slabs)


def request_rows(lens, tokens):
    start = jnp.int32(0)
    found = jnp.zeros_like(tokens)
    for r in range(lens.shape[1]):
        found = jnp.where(tokens >= start, start, found)
        start = start + lens[0, r]
    return found


def request_start(lens, token):
    start = jnp.int32(0)
    found = jnp.int32(0)
    for r in range(lens.shape[1]):
        found = jnp.where(token >= start, start, found)
        start = start + lens[0, r]
    return found


def absorb(qm, top, acc, keys, vals, first_key, lo, span, at, tile):
    count = keys.shape[0]
    cols = slice(at, at + tile)
    heads = range(MINE)
    turned = jnp.transpose(vals)
    ones = jnp.ones((ROWS - HEAD, count), BF16)
    score = [
        jnp.dot(keys[:, 128 * (h // 2):128 * (h // 2) + 128], qm[h, :, cols], preferred_element_type=F32)
        for h in heads
    ]
    number = first_key + lax.broadcasted_iota(jnp.int32, (count, tile), 0)
    allowed = number >= lo
    if span is not None:
        allowed = allowed & (number - lo <= span)
    score = [jnp.where(allowed, s, NEVER) for s in score]
    old = [top[h:h + 1, cols] for h in heads]
    new = [jnp.maximum(o, jnp.max(s, axis=0, keepdims=True)) for o, s in zip(old, score)]
    weight = [jnp.exp2((s - n) * SCALE).astype(BF16) for s, n in zip(score, new)]
    factor = [jnp.exp2((o - n) * SCALE) for o, n in zip(old, new)]
    value = [jnp.concatenate([turned[h * HEAD:(h + 1) * HEAD], ones], axis=0) for h in heads]
    added = [jnp.dot(v, w, preferred_element_type=F32) for v, w in zip(value, weight)]
    held = [acc[h, :, cols] for h in heads]
    for h in heads:
        acc[h, :, cols] = held[h] * factor[h] + added[h]
    for h in heads:
        top[h:h + 1, cols] = new[h]


def over_suffix(lens, qm, top, acc, keys, vals, first_key, first_query, causal):
    tokens = qm.shape[2]
    rows = keys.shape[0]
    piece = min(rows, 256)
    for k in range(0, rows, piece):
        key = first_key + k
        spots = [(k, tokens - k)] if causal else [(at, piece) for at in range(0, tokens, piece)]
        for at, tile in spots:
            query = first_query + at
            least = jnp.maximum(request_start(lens, query), query - (WIN - 1))

            @pl.when(key + piece > least)
            def _():
                token = query + lax.broadcasted_iota(jnp.int32, (1, tile), 1)
                lo = jnp.maximum(request_rows(lens, token), token - (WIN - 1))
                absorb(qm, top, acc, keys[k:k + piece], vals[k:k + piece], key, lo, token - lo, at, tile)


def over_prefix(lens, qm, top, acc, keys, vals, first_key, valid, first_query):
    tokens = qm.shape[2]
    rows = keys.shape[0]
    start, last = request_start(lens, first_query), request_start(lens, first_query + tokens - 1)
    least = jnp.where(start == last, first_query - start, 0)

    @pl.when(valid & (first_key + rows - 1 > least))
    def _():
        token = first_query + lax.broadcasted_iota(jnp.int32, (1, tokens), 1)
        off = token - request_rows(lens, token)
        absorb(qm, top, acc, keys[...], vals[...], first_key, off + 1, None, 0, tokens)


def begin_kernel(lens, s0, s1, s2, s3, own, qm, top, acc, held):
    block, _ = place()
    tokens = held.shape[0]
    rows = tokens // SUB
    in_order((s0, s1, s2, s3), s0.shape[0] - rows, rows, held)
    turned = jnp.transpose(held[...])
    for h in range(MINE):
        mine, other = HEAD * (h % 2), HEAD * (1 - h % 2)
        qm[h, mine:mine + HEAD, :] = turned[h * HEAD:(h + 1) * HEAD]
        qm[h, other:other + HEAD, :] = jnp.zeros((HEAD, tokens), BF16)
    top[...] = jnp.full(top.shape, LOW, F32)
    acc[...] = jnp.zeros(acc.shape, F32)
    over_prefix(lens, qm, top, acc, own.at[0], own.at[1], block * own.shape[1], True, block * tokens)


def begin(lengths, slabs, own, rows):
    tokens = rows * SUB
    scores = tokens * own.shape[1] * MINE
    return pl.pallas_call(
        begin_kernel,
        out_shape=[
            jax.ShapeDtypeStruct((MINE, 2 * HEAD, tokens), BF16),
            jax.ShapeDtypeStruct((8, tokens), F32),
            jax.ShapeDtypeStruct((MINE, ROWS, tokens), F32),
        ],
        in_specs=[pl.BlockSpec(memory_space=pltpu.SMEM)] + vmem(SUB + 1),
        out_specs=vmem(3),
        scratch_shapes=[pltpu.VMEM((tokens, WIDE), BF16)],
        compiler_params=params(),
        cost_estimate=cost(4 * HEAD * scores, 4 << 20, scores),
        name="begin",
    )(lengths, *slabs, own)


def pieces_step(sources, lens, qm, top, acc, refs, first):
    block, _ = place()
    blocks = lax.axis_size("req") // SUB
    for ref, source in zip(refs, sources):
        number = source(block)
        valid = (number >= 0) & (number < blocks)
        over_prefix(lens, qm, top, acc, ref.at[0], ref.at[1], number * ref.shape[1], valid, first)


def pieces_kernel(sources, lens, qm, top_in, acc_in, *refs):
    *refs, top, acc = refs
    top[...] = top_in[...]
    acc[...] = acc_in[...]
    block, _ = place()
    pieces_step(sources, lens, qm, top, acc, refs, block * qm.shape[2])


def suffix_kernel(distances, lens, qm, top_in, acc_in, *refs):
    *slabs, top, acc, held = refs
    block, _ = place()
    tokens = qm.shape[2]
    rows = tokens // SUB
    top[...] = top_in[...]
    acc[...] = acc_in[...]
    if len(slabs) < SUB:
        half = slabs[0].shape[0]
        slabs = [*slabs, slabs[2].at[pl.ds(half, half)]]
    for number, distance in enumerate(distances):
        for part in range(2):
            in_order(slabs, (2 * number + part) * rows, rows, held.at[part])
        first = (block - distance) * tokens
        over_suffix(lens, qm, top, acc, held.at[0], held.at[1], first, block * tokens, distance == 0)


def last_kernel(sources, other, lens, qm_in, top_in, acc_in, *refs):
    *refs, straight, cross, qm, top, acc, turned = refs
    block, sub = place()
    half = top.shape[1]
    at = jnp.bitwise_xor(sub // 2, other) * half
    cols = pl.ds(pl.multiple_of(at, half), half)
    qm[...] = qm_in[:, :, cols]
    top[...] = top_in[:, cols]
    acc[...] = acc_in[:, :, cols]
    pieces_step(sources, lens, qm, top, acc, refs, block * 2 * half + at)
    whole = jnp.concatenate([acc[h, :HEAD] * (1.0 / acc[h, HEAD:HEAD + 1]) for h in range(MINE)], axis=0)
    turned[...] = jnp.transpose(whole.astype(BF16))
    rows = straight.shape[0]
    for side, ref in enumerate((straight, cross)):
        ref[...] = turned[pl.ds(pl.multiple_of(jnp.bitwise_xor(sub % 2, side) * rows, rows), rows)]


def carry_call(kernel, name, lengths, qm, top, acc, pieces, scratch, keys):
    scores = qm.shape[2] * keys * MINE
    return pl.pallas_call(
        kernel,
        out_shape=[jax.ShapeDtypeStruct(a.shape, a.dtype) for a in (top, acc)],
        in_specs=[pl.BlockSpec(memory_space=pltpu.SMEM)] + vmem(3 + len(pieces)),
        out_specs=vmem(2),
        scratch_shapes=scratch,
        compiler_params=params(),
        cost_estimate=cost(4 * HEAD * scores, 3 << 20, scores),
        name=name,
    )(lengths, qm, top, acc, *pieces)


def prefix_call(lengths, qm, top, acc, pieces):
    return carry_call(
        functools.partial(pieces_kernel, [p[1] for p in pieces]), "prefix", lengths, qm, top, acc,
        [p[0] for p in pieces], [], sum(p[0].shape[1] for p in pieces),
    )


def suffix_call(distances, lengths, qm, top, acc, slabs):
    tokens = qm.shape[2]
    return carry_call(
        functools.partial(suffix_kernel, distances), "suffix", lengths, qm, top, acc, slabs,
        [pltpu.VMEM((2, tokens, WIDE), BF16)], tokens * len(distances),
    )


def finish(other, lengths, qm, top, acc, pieces):
    half = qm.shape[2] // 2
    rows = half // 2
    scores = half * sum(p[0].shape[1] for p in pieces) * MINE
    return pl.pallas_call(
        functools.partial(last_kernel, [p[1] for p in pieces], other),
        out_shape=[jax.ShapeDtypeStruct((rows, WIDE), BF16)] * 2,
        in_specs=[pl.BlockSpec(memory_space=pltpu.SMEM)] + vmem(3 + len(pieces)),
        out_specs=vmem(2),
        scratch_shapes=[
            pltpu.VMEM((MINE, 2 * HEAD, half), BF16),
            pltpu.VMEM((8, half), F32),
            pltpu.VMEM((MINE, ROWS, half), F32),
            pltpu.VMEM((half, WIDE), BF16),
        ],
        compiler_params=params(),
        cost_estimate=cost(4 * HEAD * scores, 2 << 20, scores),
        name="last",
    )(lengths, qm, top, acc, *[p[0] for p in pieces])


def join_kernel(s0, s1, s2, s3, out):
    _, sub = place()
    for distance, ref in enumerate((s0, s1, s2, s3)):
        out[0, :, columns(partner(sub, distance))] = ref[...]


def join(slabs):
    rows = slabs[0].shape[0]
    return pl.pallas_call(
        join_kernel,
        out_shape=jax.ShapeDtypeStruct((1, rows, WIDE * SUB), BF16),
        in_specs=vmem(SUB),
        out_specs=vmem(1)[0],
        compiler_params=params(),
        cost_estimate=cost(0, 4 * rows * WIDE * SUB),
        name="join",
    )(*slabs)


def on_device(queries, suffix_kv, prefix_kv, lengths):
    rows = queries.shape[1]
    count = lax.axis_size("req")
    blocks = count // SUB
    tokens = rows * SUB
    longest = count * rows // 4
    reach = -(-(min(WIN, longest) - 1) // tokens)
    reach = min(reach, blocks - 1)

    raw = [shift(suffix_kv, d) for d in range(1, reach + 1)]
    slabs = exchange(cut(prefix_kv, queries[:, None]), 2)
    near = trade(suffix_kv)
    own = lay(slabs, prefix_kv.shape[2])
    qm, top, acc = begin(lengths, slabs, own, rows)
    pieces = gather_four(own, top) if blocks == 4 else gather_row(own, blocks)
    top, acc = suffix_call([0], lengths, qm, top, acc, near)
    halo = [exchange(cut(r)) for r in raw]
    if blocks == 4:
        two, where = pieces[-1]
        two, top, _ = lax.optimization_barrier((two, top, [h[2:] for h in halo]))
        pieces = pieces[:-1] + [(two, where), pass_on(two)]
    for back in range(1, reach + 1):
        top, acc = suffix_call([back], lengths, qm, top, acc, halo[back - 1])
    top, acc = prefix_call(lengths, qm, top, acc, pieces[:3])
    far = finish(1, lengths, qm, top, acc, pieces[3:])
    near = finish(0, lengths, qm, top, acc, pieces[3:])
    return join(exchange([*near, *far]))


def solution(mesh):
    in_specs = (
        P("grp", "req", None),
        P("grp", None, "req", None),
        P("grp", None, "req", None),
        P("grp", None),
    )
    out_specs = P("grp", "req", None)
    return jax.shard_map(
        on_device, mesh=mesh, in_specs=in_specs, out_specs=out_specs, check_vma=False
    )
```

```python
import functools
import math

import jax
import jax.numpy as jnp
from jax import lax
from jax.experimental import pallas as pl
from jax.experimental.pallas import tpu as pltpu
from jax.sharding import PartitionSpec as P

HEADS = 16
HEAD = 64
WIN = 1024
SUB = 4
MINE = HEADS // SUB
WIDE = MINE * HEAD
ROWS = HEAD + 16
SCALE = 0.125 * math.log2(math.e)
LOW = -8e30
NEVER = -3e38

BF16 = jnp.bfloat16
F32 = jnp.float32


def place():
    position = lax.axis_index("req")
    return position // SUB, position % SUB


def partner(sub, distance):
    return jnp.bitwise_xor(sub, distance)


def columns(owner):
    return pl.ds(pl.multiple_of(owner * WIDE, WIDE), WIDE)


def params():
    return pltpu.CompilerParams(vmem_limit_bytes=48 * 1024 * 1024)


def vmem(count):
    return [pl.BlockSpec(memory_space=pltpu.VMEM)] * count


def cost(flops, moved, exps=0):
    return pl.CostEstimate(flops=flops, bytes_accessed=moved, transcendentals=exps)


def cut_kernel(*refs):
    ins, outs = refs[:-SUB], refs[-SUB:]
    _, sub = place()
    for distance, out in enumerate(outs):
        cols = columns(partner(sub, distance))
        at = 0
        for ref in ins:
            rows = ref.shape[2]
            for part in range(ref.shape[1]):
                out[at:at + rows] = ref[0, part, :, cols]
                at += rows


def cut(*arrays):
    rows = sum(a.shape[1] * a.shape[2] for a in arrays)
    return pl.pallas_call(
        cut_kernel,
        out_shape=[jax.ShapeDtypeStruct((rows, WIDE), BF16)] * SUB,
        in_specs=vmem(len(arrays)),
        out_specs=vmem(SUB),
        compiler_params=params(),
        cost_estimate=cost(0, 4 * SUB * rows * WIDE),
        name="cut",
    )(*arrays)


def exchange(slabs, nearest_after=None):
    count = lax.axis_size("req")
    got = {0: slabs[0]}
    for distance in (2, 3, 1):
        slab = slabs[distance]
        if distance == 1 and nearest_after is not None:
            slab, _ = lax.optimization_barrier((slab, got[nearest_after]))
        got[distance] = lax.ppermute(slab, "req", [(i, i ^ distance) for i in range(count)])
    return [got[distance] for distance in range(SUB)]


def between(block, routes):
    return lax.ppermute(block, "req", [(SUB * a + s, SUB * b + s) for a, b in routes for s in range(SUB)])


def shift(block, blocks, since=0):
    last = lax.axis_size("req") // SUB - 1
    low, high = (since, last - blocks) if blocks > 0 else (-blocks, last - since)
    return between(block, [(b, b + blocks) for b in range(low, high + 1)])


def gather_four(own, top):
    two = between(own, [(0, 2), (2, 0), (1, 3), (3, 1)])
    one = between(own, [(0, 1), (1, 0), (2, 3), (3, 2)])
    middle = between(own, [(1, 2), (2, 1)])
    return [
        (one, lambda b: jnp.bitwise_xor(b, 1)),
        (middle, lambda b: jnp.where((b == 1) | (b == 2), 3 - b, -1)),
        (two, lambda b: jnp.bitwise_xor(b, 2)),
    ]


def pass_on(two):
    ends = between(two, [(2, 3), (1, 0)])
    return ends, lambda b: jnp.where((b == 0) | (b == 3), 3 - b, -1)


def gather_row(own, blocks):
    pieces = []
    left = right = own
    for distance in range(1, blocks):
        left, right = shift(left, 1, distance - 1), shift(right, -1, distance - 1)
        pieces.append((left, lambda b, d=distance: b - d))
        pieces.append((right, lambda b, d=distance: b + d))
    return pieces


def in_order(slabs, first, rows, out):
    _, sub = place()
    for distance, ref in enumerate(slabs):
        at = pl.ds(pl.multiple_of(partner(sub, distance) * rows, rows), rows)
        out[at, :] = ref[first:first + rows]


def deal_kernel(*refs):
    ins, (own, near, far) = refs[:-3], refs[-3:]
    _, sub = place()
    half = own.shape[0]
    for distance, (out, at) in enumerate(((own, 0), (near, 0), (far, 0), (near, half))):
        cols = columns(partner(sub, distance))
        for ref in ins:
            rows = ref.shape[2]
            for part in range(ref.shape[1]):
                out[at:at + rows] = ref[0, part, :, cols]
                at += rows


def pair_kernel(far, near, out):
    rows = far.shape[0]
    out[:rows] = far[...]
    out[rows:] = near[rows:]


def trade(*arrays, after=None):
    rows = sum(a.shape[1] * a.shape[2] for a in arrays)
    slab = jax.ShapeDtypeStruct((rows, WIDE), BF16)
    slabs = jax.ShapeDtypeStruct((2 * rows, WIDE), BF16)
    own, near, far = pl.pallas_call(
        deal_kernel,
        out_shape=[slab, slabs, slab],
        in_specs=vmem(len(arrays)),
        out_specs=vmem(3),
        compiler_params=params(),
        cost_estimate=cost(0, 4 * SUB * rows * WIDE),
        name="deal",
    )(*arrays)
    count = lax.axis_size("req")
    near = lax.ppermute(near, "req", [(i, i ^ 1) for i in range(count)])
    if after is not None:
        near, _ = lax.optimization_barrier((near, after))
    far = pl.pallas_call(
        pair_kernel,
        out_shape=slabs,
        in_specs=vmem(2),
        out_specs=vmem(1)[0],
        compiler_params=params(),
        cost_estimate=cost(0, 8 * rows * WIDE),
        name="pair",
    )(far, near)
    return own, near, lax.ppermute(far, "req", [(i, i ^ 2) for i in range(count)])


def lay_kernel(*refs):
    *slabs, out = refs
    rows = out.shape[1] // SUB
    for part in range(2):
        in_order(slabs, part * rows, rows, out.at[part])


def lay(slabs, rows):
    return pl.pallas_call(
        lay_kernel,
        out_shape=jax.ShapeDtypeStruct((2, rows * SUB, WIDE), BF16),
        in_specs=vmem(SUB),
        out_specs=vmem(1)[0],
        compiler_params=params(),
        cost_estimate=cost(0, 8 * SUB * rows * WIDE),
        name="lay",
    )(*slabs)


def request_rows(lens, tokens):
    start = jnp.int32(0)
    found = jnp.zeros_like(tokens)
    for r in range(lens.shape[1]):
        found = jnp.where(tokens >= start, start, found)
        start = start + lens[0, r]
    return found


def request_start(lens, token):
    start = jnp.int32(0)
    found = jnp.int32(0)
    for r in range(lens.shape[1]):
        found = jnp.where(token >= start, start, found)
        start = start + lens[0, r]
    return found


def absorb(qm, top, acc, keys, vals, first_key, lo, span, at, tile):
    count = keys.shape[0]
    cols = slice(at, at + tile)
    heads = range(MINE)
    turned = jnp.transpose(vals)
    ones = jnp.ones((ROWS - HEAD, count), BF16)
    score = [
        jnp.dot(keys[:, 128 * (h // 2):128 * (h // 2) + 128], qm[h, :, cols], preferred_element_type=F32)
        for h in heads
    ]
    number = first_key + lax.broadcasted_iota(jnp.int32, (count, tile), 0)
    allowed = number >= lo
    if span is not None:
        allowed = allowed & (number - lo <= span)
    score = [jnp.where(allowed, s, NEVER) for s in score]
    old = [top[h:h + 1, cols] for h in heads]
    new = [jnp.maximum(o, jnp.max(s, axis=0, keepdims=True)) for o, s in zip(old, score)]
    weight = [jnp.exp2((s - n) * SCALE).astype(BF16) for s, n in zip(score, new)]
    factor = [jnp.exp2((o - n) * SCALE) for o, n in zip(old, new)]
    value = [jnp.concatenate([turned[h * HEAD:(h + 1) * HEAD], ones], axis=0) for h in heads]
    added = [jnp.dot(v, w, preferred_element_type=F32) for v, w in zip(value, weight)]
    held = [acc[h, :, cols] for h in heads]
    for h in heads:
        acc[h, :, cols] = held[h] * factor[h] + added[h]
    for h in heads:
        top[h:h + 1, cols] = new[h]


def over_suffix(lens, qm, top, acc, keys, vals, first_key, first_query, causal):
    tokens = qm.shape[2]
    rows = keys.shape[0]
    piece = min(rows, 256)
    for k in range(0, rows, piece):
        key = first_key + k
        spots = [(k, tokens - k)] if causal else [(at, piece) for at in range(0, tokens, piece)]
        for at, tile in spots:
            query = first_query + at
            least = jnp.maximum(request_start(lens, query), query - (WIN - 1))

            @pl.when(key + piece > least)
            def _():
                token = query + lax.broadcasted_iota(jnp.int32, (1, tile), 1)
                lo = jnp.maximum(request_rows(lens, token), token - (WIN - 1))
                absorb(qm, top, acc, keys[k:k + piece], vals[k:k + piece], key, lo, token - lo, at, tile)


def over_prefix(lens, qm, top, acc, keys, vals, first_key, valid, first_query):
    tokens = qm.shape[2]
    rows = keys.shape[0]
    start, last = request_start(lens, first_query), request_start(lens, first_query + tokens - 1)
    least = jnp.where(start == last, first_query - start, 0)

    @pl.when(valid & (first_key + rows - 1 > least))
    def _():
        token = first_query + lax.broadcasted_iota(jnp.int32, (1, tokens), 1)
        off = token - request_rows(lens, token)
        absorb(qm, top, acc, keys[...], vals[...], first_key, off + 1, None, 0, tokens)


def begin_kernel(lens, s0, s1, s2, s3, own, qm, top, acc, held):
    block, _ = place()
    tokens = held.shape[0]
    rows = tokens // SUB
    in_order((s0, s1, s2, s3), s0.shape[0] - rows, rows, held)
    turned = jnp.transpose(held[...])
    for h in range(MINE):
        mine, other = HEAD * (h % 2), HEAD * (1 - h % 2)
        qm[h, mine:mine + HEAD, :] = turned[h * HEAD:(h + 1) * HEAD]
        qm[h, other:other + HEAD, :] = jnp.zeros((HEAD, tokens), BF16)
    top[...] = jnp.full(top.shape, LOW, F32)
    acc[...] = jnp.zeros(acc.shape, F32)
    over_prefix(lens, qm, top, acc, own.at[0], own.at[1], block * own.shape[1], True, block * tokens)


def begin(lengths, slabs, own, rows):
    tokens = rows * SUB
    scores = tokens * own.shape[1] * MINE
    return pl.pallas_call(
        begin_kernel,
        out_shape=[
            jax.ShapeDtypeStruct((MINE, 2 * HEAD, tokens), BF16),
            jax.ShapeDtypeStruct((8, tokens), F32),
            jax.ShapeDtypeStruct((MINE, ROWS, tokens), F32),
        ],
        in_specs=[pl.BlockSpec(memory_space=pltpu.SMEM)] + vmem(SUB + 1),
        out_specs=vmem(3),
        scratch_shapes=[pltpu.VMEM((tokens, WIDE), BF16)],
        compiler_params=params(),
        cost_estimate=cost(4 * HEAD * scores, 4 << 20, scores),
        name="begin",
    )(lengths, *slabs, own)


def pieces_step(sources, lens, qm, top, acc, refs, first):
    block, _ = place()
    blocks = lax.axis_size("req") // SUB
    for ref, source in zip(refs, sources):
        number = source(block)
        valid = (number >= 0) & (number < blocks)
        over_prefix(lens, qm, top, acc, ref.at[0], ref.at[1], number * ref.shape[1], valid, first)


def pieces_kernel(sources, lens, qm, top_in, acc_in, *refs):
    *refs, top, acc = refs
    top[...] = top_in[...]
    acc[...] = acc_in[...]
    block, _ = place()
    pieces_step(sources, lens, qm, top, acc, refs, block * qm.shape[2])


def suffix_kernel(distances, lens, qm, top_in, acc_in, *refs):
    *slabs, top, acc, held = refs
    block, _ = place()
    tokens = qm.shape[2]
    rows = tokens // SUB
    top[...] = top_in[...]
    acc[...] = acc_in[...]
    if len(slabs) < SUB:
        half = slabs[0].shape[0]
        slabs = [*slabs, slabs[2].at[pl.ds(half, half)]]
    for number, distance in enumerate(distances):
        for part in range(2):
            in_order(slabs, (2 * number + part) * rows, rows, held.at[part])
        first = (block - distance) * tokens
        over_suffix(lens, qm, top, acc, held.at[0], held.at[1], first, block * tokens, distance == 0)


def last_kernel(sources, other, lens, qm_in, top_in, acc_in, *refs):
    *refs, straight, cross, qm, top, acc, turned = refs
    block, sub = place()
    half = top.shape[1]
    at = jnp.bitwise_xor(sub // 2, other) * half
    cols = pl.ds(pl.multiple_of(at, half), half)
    qm[...] = qm_in[:, :, cols]
    top[...] = top_in[:, cols]
    acc[...] = acc_in[:, :, cols]
    pieces_step(sources, lens, qm, top, acc, refs, block * 2 * half + at)
    whole = jnp.concatenate([acc[h, :HEAD] * (1.0 / acc[h, HEAD:HEAD + 1]) for h in range(MINE)], axis=0)
    turned[...] = jnp.transpose(whole.astype(BF16))
    rows = straight.shape[0]
    for side, ref in enumerate((straight, cross)):
        ref[...] = turned[pl.ds(pl.multiple_of(jnp.bitwise_xor(sub % 2, side) * rows, rows), rows)]


def carry_call(kernel, name, lengths, qm, top, acc, pieces, scratch, keys):
    scores = qm.shape[2] * keys * MINE
    return pl.pallas_call(
        kernel,
        out_shape=[jax.ShapeDtypeStruct(a.shape, a.dtype) for a in (top, acc)],
        in_specs=[pl.BlockSpec(memory_space=pltpu.SMEM)] + vmem(3 + len(pieces)),
        out_specs=vmem(2),
        scratch_shapes=scratch,
        compiler_params=params(),
        cost_estimate=cost(4 * HEAD * scores, 3 << 20, scores),
        name=name,
    )(lengths, qm, top, acc, *pieces)


def prefix_call(lengths, qm, top, acc, pieces):
    return carry_call(
        functools.partial(pieces_kernel, [p[1] for p in pieces]), "prefix", lengths, qm, top, acc,
        [p[0] for p in pieces], [], sum(p[0].shape[1] for p in pieces),
    )


def suffix_call(distances, lengths, qm, top, acc, slabs):
    tokens = qm.shape[2]
    return carry_call(
        functools.partial(suffix_kernel, distances), "suffix", lengths, qm, top, acc, slabs,
        [pltpu.VMEM((2, tokens, WIDE), BF16)], tokens * len(distances),
    )


def finish(other, lengths, qm, top, acc, pieces):
    half = qm.shape[2] // 2
    rows = half // 2
    scores = half * sum(p[0].shape[1] for p in pieces) * MINE
    return pl.pallas_call(
        functools.partial(last_kernel, [p[1] for p in pieces], other),
        out_shape=[jax.ShapeDtypeStruct((rows, WIDE), BF16)] * 2,
        in_specs=[pl.BlockSpec(memory_space=pltpu.SMEM)] + vmem(3 + len(pieces)),
        out_specs=vmem(2),
        scratch_shapes=[
            pltpu.VMEM((MINE, 2 * HEAD, half), BF16),
            pltpu.VMEM((8, half), F32),
            pltpu.VMEM((MINE, ROWS, half), F32),
            pltpu.VMEM((half, WIDE), BF16),
        ],
        compiler_params=params(),
        cost_estimate=cost(4 * HEAD * scores, 2 << 20, scores),
        name="last",
    )(lengths, qm, top, acc, *[p[0] for p in pieces])


def join_kernel(s0, s1, s2, s3, out):
    _, sub = place()
    for distance, ref in enumerate((s0, s1, s2, s3)):
        out[0, :, columns(partner(sub, distance))] = ref[...]


def join(slabs):
    rows = slabs[0].shape[0]
    return pl.pallas_call(
        join_kernel,
        out_shape=jax.ShapeDtypeStruct((1, rows, WIDE * SUB), BF16),
        in_specs=vmem(SUB),
        out_specs=vmem(1)[0],
        compiler_params=params(),
        cost_estimate=cost(0, 4 * rows * WIDE * SUB),
        name="join",
    )(*slabs)


def on_device(queries, suffix_kv, prefix_kv, lengths):
    rows = queries.shape[1]
    count = lax.axis_size("req")
    blocks = count // SUB
    tokens = rows * SUB
    longest = count * rows // 4
    reach = -(-(min(WIN, longest) - 1) // tokens)
    reach = min(reach, blocks - 1)

    raw = [shift(suffix_kv, d) for d in range(1, reach + 1)]
    slabs = exchange(cut(prefix_kv, queries[:, None]), 2)
    near = trade(suffix_kv)
    own = lay(slabs, prefix_kv.shape[2])
    qm, top, acc = begin(lengths, slabs, own, rows)
    pieces = gather_four(own, top) if blocks == 4 else gather_row(own, blocks)
    top, acc = suffix_call([0], lengths, qm, top, acc, near)
    halo = [exchange(cut(r)) for r in raw]
    if blocks == 4:
        two, where = pieces[-1]
        two, top, _ = lax.optimization_barrier((two, top, [h[2:] for h in halo]))
        pieces = pieces[:-1] + [(two, where), pass_on(two)]
    for back in range(1, reach + 1):
        top, acc = suffix_call([back], lengths, qm, top, acc, halo[back - 1])
    top, acc = prefix_call(lengths, qm, top, acc, pieces[:3])
    far = finish(1, lengths, qm, top, acc, pieces[3:])
    near = finish(0, lengths, qm, top, acc, pieces[3:])
    return join(exchange([*near, *far]))


def solution(mesh):
    in_specs = (
        P("grp", "req", None),
        P("grp", None, "req", None),
        P("grp", None, "req", None),
        P("grp", None),
    )
    out_specs = P("grp", "req", None)
    return jax.shard_map(
        on_device, mesh=mesh, in_specs=in_specs, out_specs=out_specs, check_vma=False
    )
```

```python
import functools
import math

import jax
import jax.numpy as jnp
from jax import lax
from jax.experimental import pallas as pl
from jax.experimental.pallas import tpu as pltpu
from jax.sharding import PartitionSpec as P

HEADS = 16
HEAD = 64
WIN = 1024
SUB = 4
MINE = HEADS // SUB
WIDE = MINE * HEAD
ROWS = HEAD + 16
SCALE = 0.125 * math.log2(math.e)
LOW = -8e30
NEVER = -3e38

BF16 = jnp.bfloat16
F32 = jnp.float32


def place():
    position = lax.axis_index("req")
    return position // SUB, position % SUB


def partner(sub, distance):
    return jnp.bitwise_xor(sub, distance)


def columns(owner):
    return pl.ds(pl.multiple_of(owner * WIDE, WIDE), WIDE)


def params():
    return pltpu.CompilerParams(vmem_limit_bytes=48 * 1024 * 1024)


def vmem(count):
    return [pl.BlockSpec(memory_space=pltpu.VMEM)] * count


def cost(flops, moved, exps=0):
    return pl.CostEstimate(flops=flops, bytes_accessed=moved, transcendentals=exps)


def cut_kernel(*refs):
    ins, outs = refs[:-SUB], refs[-SUB:]
    _, sub = place()
    for distance, out in enumerate(outs):
        cols = columns(partner(sub, distance))
        at = 0
        for ref in ins:
            rows = ref.shape[2]
            for part in range(ref.shape[1]):
                out[at:at + rows] = ref[0, part, :, cols]
                at += rows


def cut(*arrays):
    rows = sum(a.shape[1] * a.shape[2] for a in arrays)
    return pl.pallas_call(
        cut_kernel,
        out_shape=[jax.ShapeDtypeStruct((rows, WIDE), BF16)] * SUB,
        in_specs=vmem(len(arrays)),
        out_specs=vmem(SUB),
        compiler_params=params(),
        cost_estimate=cost(0, 4 * SUB * rows * WIDE),
        name="cut",
    )(*arrays)


def exchange(slabs, nearest_after=None):
    count = lax.axis_size("req")
    got = {0: slabs[0]}
    for distance in (2, 3, 1):
        slab = slabs[distance]
        if distance == 1 and nearest_after is not None:
            slab, _ = lax.optimization_barrier((slab, got[nearest_after]))
        got[distance] = lax.ppermute(slab, "req", [(i, i ^ distance) for i in range(count)])
    return [got[distance] for distance in range(SUB)]


def between(block, routes):
    return lax.ppermute(block, "req", [(SUB * a + s, SUB * b + s) for a, b in routes for s in range(SUB)])


def shift(block, blocks, since=0):
    last = lax.axis_size("req") // SUB - 1
    low, high = (since, last - blocks) if blocks > 0 else (-blocks, last - since)
    return between(block, [(b, b + blocks) for b in range(low, high + 1)])


def gather_four(own, top):
    two = between(own, [(0, 2), (2, 0), (1, 3), (3, 1)])
    one = between(own, [(0, 1), (1, 0), (2, 3), (3, 2)])
    middle = between(own, [(1, 2), (2, 1)])
    return [
        (one, lambda b: jnp.bitwise_xor(b, 1)),
        (middle, lambda b: jnp.where((b == 1) | (b == 2), 3 - b, -1)),
        (two, lambda b: jnp.bitwise_xor(b, 2)),
    ]


def pass_on(two):
    ends = between(two, [(2, 3), (1, 0)])
    return ends, lambda b: jnp.where((b == 0) | (b == 3), 3 - b, -1)


def gather_row(own, blocks):
    pieces = []
    left = right = own
    for distance in range(1, blocks):
        left, right = shift(left, 1, distance - 1), shift(right, -1, distance - 1)
        pieces.append((left, lambda b, d=distance: b - d))
        pieces.append((right, lambda b, d=distance: b + d))
    return pieces


def in_order(slabs, first, rows, out):
    _, sub = place()
    for distance, ref in enumerate(slabs):
        at = pl.ds(pl.multiple_of(partner(sub, distance) * rows, rows), rows)
        out[at, :] = ref[first:first + rows]


def deal_kernel(*refs):
    ins, (own, near, far) = refs[:-3], refs[-3:]
    _, sub = place()
    half = own.shape[0]
    for distance, (out, at) in enumerate(((own, 0), (near, 0), (far, 0), (near, half))):
        cols = columns(partner(sub, distance))
        for ref in ins:
            rows = ref.shape[2]
            for part in range(ref.shape[1]):
                out[at:at + rows] = ref[0, part, :, cols]
                at += rows


def pair_kernel(far, near, out):
    rows = far.shape[0]
    out[:rows] = far[...]
    out[rows:] = near[rows:]


def trade(*arrays, after=None):
    rows = sum(a.shape[1] * a.shape[2] for a in arrays)
    slab = jax.ShapeDtypeStruct((rows, WIDE), BF16)
    slabs = jax.ShapeDtypeStruct((2 * rows, WIDE), BF16)
    own, near, far = pl.pallas_call(
        deal_kernel,
        out_shape=[slab, slabs, slab],
        in_specs=vmem(len(arrays)),
        out_specs=vmem(3),
        compiler_params=params(),
        cost_estimate=cost(0, 4 * SUB * rows * WIDE),
        name="deal",
    )(*arrays)
    count = lax.axis_size("req")
    near = lax.ppermute(near, "req", [(i, i ^ 1) for i in range(count)])
    if after is not None:
        near, _ = lax.optimization_barrier((near, after))
    far = pl.pallas_call(
        pair_kernel,
        out_shape=slabs,
        in_specs=vmem(2),
        out_specs=vmem(1)[0],
        compiler_params=params(),
        cost_estimate=cost(0, 8 * rows * WIDE),
        name="pair",
    )(far, near)
    return own, near, lax.ppermute(far, "req", [(i, i ^ 2) for i in range(count)])


def lay_kernel(*refs):
    *slabs, out = refs
    rows = out.shape[1] // SUB
    for part in range(2):
        in_order(slabs, part * rows, rows, out.at[part])


def lay(slabs, rows):
    return pl.pallas_call(
        lay_kernel,
        out_shape=jax.ShapeDtypeStruct((2, rows * SUB, WIDE), BF16),
        in_specs=vmem(SUB),
        out_specs=vmem(1)[0],
        compiler_params=params(),
        cost_estimate=cost(0, 8 * SUB * rows * WIDE),
        name="lay",
    )(*slabs)


def request_rows(lens, tokens):
    start = jnp.int32(0)
    found = jnp.zeros_like(tokens)
    for r in range(lens.shape[1]):
        found = jnp.where(tokens >= start, start, found)
        start = start + lens[0, r]
    return found


def request_start(lens, token):
    start = jnp.int32(0)
    found = jnp.int32(0)
    for r in range(lens.shape[1]):
        found = jnp.where(token >= start, start, found)
        start = start + lens[0, r]
    return found


def absorb(qm, top, acc, keys, vals, first_key, lo, span, at, tile):
    count = keys.shape[0]
    cols = slice(at, at + tile)
    heads = range(MINE)
    turned = jnp.transpose(vals)
    ones = jnp.ones((ROWS - HEAD, count), BF16)
    score = [
        jnp.dot(keys[:, 128 * (h // 2):128 * (h // 2) + 128], qm[h, :, cols], preferred_element_type=F32)
        for h in heads
    ]
    number = first_key + lax.broadcasted_iota(jnp.int32, (count, tile), 0)
    allowed = number >= lo
    if span is not None:
        allowed = allowed & (number - lo <= span)
    score = [jnp.where(allowed, s, NEVER) for s in score]
    old = [top[h:h + 1, cols] for h in heads]
    new = [jnp.maximum(o, jnp.max(s, axis=0, keepdims=True)) for o, s in zip(old, score)]
    weight = [jnp.exp2((s - n) * SCALE).astype(BF16) for s, n in zip(score, new)]
    factor = [jnp.exp2((o - n) * SCALE) for o, n in zip(old, new)]
    value = [jnp.concatenate([turned[h * HEAD:(h + 1) * HEAD], ones], axis=0) for h in heads]
    added = [jnp.dot(v, w, preferred_element_type=F32) for v, w in zip(value, weight)]
    held = [acc[h, :, cols] for h in heads]
    for h in heads:
        acc[h, :, cols] = held[h] * factor[h] + added[h]
    for h in heads:
        top[h:h + 1, cols] = new[h]


def over_suffix(lens, qm, top, acc, keys, vals, first_key, first_query, causal):
    tokens = qm.shape[2]
    rows = keys.shape[0]
    piece = min(rows, 256)
    for k in range(0, rows, piece):
        key = first_key + k
        spots = [(k, tokens - k)] if causal else [(at, piece) for at in range(0, tokens, piece)]
        for at, tile in spots:
            query = first_query + at
            least = jnp.maximum(request_start(lens, query), query - (WIN - 1))

            @pl.when(key + piece > least)
            def _():
                token = query + lax.broadcasted_iota(jnp.int32, (1, tile), 1)
                lo = jnp.maximum(request_rows(lens, token), token - (WIN - 1))
                absorb(qm, top, acc, keys[k:k + piece], vals[k:k + piece], key, lo, token - lo, at, tile)


def over_prefix(lens, qm, top, acc, keys, vals, first_key, valid, first_query):
    tokens = qm.shape[2]
    rows = keys.shape[0]
    start, last = request_start(lens, first_query), request_start(lens, first_query + tokens - 1)
    least = jnp.where(start == last, first_query - start, 0)

    @pl.when(valid & (first_key + rows - 1 > least))
    def _():
        token = first_query + lax.broadcasted_iota(jnp.int32, (1, tokens), 1)
        off = token - request_rows(lens, token)
        absorb(qm, top, acc, keys[...], vals[...], first_key, off + 1, None, 0, tokens)


def begin_kernel(lens, s0, s1, s2, s3, own, qm, top, acc, held):
    block, _ = place()
    tokens = held.shape[0]
    rows = tokens // SUB
    in_order((s0, s1, s2, s3), s0.shape[0] - rows, rows, held)
    turned = jnp.transpose(held[...])
    for h in range(MINE):
        mine, other = HEAD * (h % 2), HEAD * (1 - h % 2)
        qm[h, mine:mine + HEAD, :] = turned[h * HEAD:(h + 1) * HEAD]
        qm[h, other:other + HEAD, :] = jnp.zeros((HEAD, tokens), BF16)
    top[...] = jnp.full(top.shape, LOW, F32)
    acc[...] = jnp.zeros(acc.shape, F32)
    over_prefix(lens, qm, top, acc, own.at[0], own.at[1], block * own.shape[1], True, block * tokens)


def begin(lengths, slabs, own, rows):
    tokens = rows * SUB
    scores = tokens * own.shape[1] * MINE
    return pl.pallas_call(
        begin_kernel,
        out_shape=[
            jax.ShapeDtypeStruct((MINE, 2 * HEAD, tokens), BF16),
            jax.ShapeDtypeStruct((8, tokens), F32),
            jax.ShapeDtypeStruct((MINE, ROWS, tokens), F32),
        ],
        in_specs=[pl.BlockSpec(memory_space=pltpu.SMEM)] + vmem(SUB + 1),
        out_specs=vmem(3),
        scratch_shapes=[pltpu.VMEM((tokens, WIDE), BF16)],
        compiler_params=params(),
        cost_estimate=cost(4 * HEAD * scores, 4 << 20, scores),
        name="begin",
    )(lengths, *slabs, own)


def pieces_step(sources, lens, qm, top, acc, refs, first):
    block, _ = place()
    blocks = lax.axis_size("req") // SUB
    for ref, source in zip(refs, sources):
        number = source(block)
        valid = (number >= 0) & (number < blocks)
        over_prefix(lens, qm, top, acc, ref.at[0], ref.at[1], number * ref.shape[1], valid, first)


def pieces_kernel(sources, lens, qm, top_in, acc_in, *refs):
    *refs, top, acc = refs
    top[...] = top_in[...]
    acc[...] = acc_in[...]
    block, _ = place()
    pieces_step(sources, lens, qm, top, acc, refs, block * qm.shape[2])


def suffix_kernel(distances, lens, qm, top_in, acc_in, *refs):
    *slabs, top, acc, held = refs
    block, _ = place()
    tokens = qm.shape[2]
    rows = tokens // SUB
    top[...] = top_in[...]
    acc[...] = acc_in[...]
    if len(slabs) < SUB:
        half = slabs[0].shape[0]
        slabs = [*slabs, slabs[2].at[pl.ds(half, half)]]
    for number, distance in enumerate(distances):
        for part in range(2):
            in_order(slabs, (2 * number + part) * rows, rows, held.at[part])
        first = (block - distance) * tokens
        over_suffix(lens, qm, top, acc, held.at[0], held.at[1], first, block * tokens, distance == 0)


def last_kernel(sources, other, lens, qm_in, top_in, acc_in, *refs):
    *refs, straight, cross, top, acc, turned = refs
    block, sub = place()
    half = top.shape[1]
    at = jnp.bitwise_xor(sub // 2, other) * half
    cols = pl.ds(pl.multiple_of(at, half), half)
    qm = qm_in.at[:, :, cols]
    top[...] = top_in[:, cols]
    acc[...] = acc_in[:, :, cols]
    pieces_step(sources, lens, qm, top, acc, refs, block * 2 * half + at)
    whole = jnp.concatenate([acc[h, :HEAD] * (1.0 / acc[h, HEAD:HEAD + 1]) for h in range(MINE)], axis=0)
    turned[...] = jnp.transpose(whole.astype(BF16))
    rows = straight.shape[0]
    for side, ref in enumerate((straight, cross)):
        ref[...] = turned[pl.ds(pl.multiple_of(jnp.bitwise_xor(sub % 2, side) * rows, rows), rows)]


def carry_call(kernel, name, lengths, qm, top, acc, pieces, scratch, keys):
    scores = qm.shape[2] * keys * MINE
    return pl.pallas_call(
        kernel,
        out_shape=[jax.ShapeDtypeStruct(a.shape, a.dtype) for a in (top, acc)],
        in_specs=[pl.BlockSpec(memory_space=pltpu.SMEM)] + vmem(3 + len(pieces)),
        out_specs=vmem(2),
        scratch_shapes=scratch,
        compiler_params=params(),
        cost_estimate=cost(4 * HEAD * scores, 3 << 20, scores),
        name=name,
    )(lengths, qm, top, acc, *pieces)


def prefix_call(lengths, qm, top, acc, pieces):
    return carry_call(
        functools.partial(pieces_kernel, [p[1] for p in pieces]), "prefix", lengths, qm, top, acc,
        [p[0] for p in pieces], [], sum(p[0].shape[1] for p in pieces),
    )


def suffix_call(distances, lengths, qm, top, acc, slabs):
    tokens = qm.shape[2]
    return carry_call(
        functools.partial(suffix_kernel, distances), "suffix", lengths, qm, top, acc, slabs,
        [pltpu.VMEM((2, tokens, WIDE), BF16)], tokens * len(distances),
    )


def finish(other, lengths, qm, top, acc, pieces):
    half = qm.shape[2] // 2
    rows = half // 2
    scores = half * sum(p[0].shape[1] for p in pieces) * MINE
    return pl.pallas_call(
        functools.partial(last_kernel, [p[1] for p in pieces], other),
        out_shape=[jax.ShapeDtypeStruct((rows, WIDE), BF16)] * 2,
        in_specs=[pl.BlockSpec(memory_space=pltpu.SMEM)] + vmem(3 + len(pieces)),
        out_specs=vmem(2),
        scratch_shapes=[
            pltpu.VMEM((8, half), F32),
            pltpu.VMEM((MINE, ROWS, half), F32),
            pltpu.VMEM((half, WIDE), BF16),
        ],
        compiler_params=params(),
        cost_estimate=cost(4 * HEAD * scores, 2 << 20, scores),
        name="last",
    )(lengths, qm, top, acc, *[p[0] for p in pieces])


def join_kernel(s0, s1, s2, s3, out):
    _, sub = place()
    for distance, ref in enumerate((s0, s1, s2, s3)):
        out[0, :, columns(partner(sub, distance))] = ref[...]


def join(slabs):
    rows = slabs[0].shape[0]
    return pl.pallas_call(
        join_kernel,
        out_shape=jax.ShapeDtypeStruct((1, rows, WIDE * SUB), BF16),
        in_specs=vmem(SUB),
        out_specs=vmem(1)[0],
        compiler_params=params(),
        cost_estimate=cost(0, 4 * rows * WIDE * SUB),
        name="join",
    )(*slabs)


def on_device(queries, suffix_kv, prefix_kv, lengths):
    rows = queries.shape[1]
    count = lax.axis_size("req")
    blocks = count // SUB
    tokens = rows * SUB
    longest = count * rows // 4
    reach = -(-(min(WIN, longest) - 1) // tokens)
    reach = min(reach, blocks - 1)

    raw = [shift(suffix_kv, d) for d in range(1, reach + 1)]
    slabs = exchange(cut(prefix_kv, queries[:, None]), 2)
    near = trade(suffix_kv)
    own = lay(slabs, prefix_kv.shape[2])
    qm, top, acc = begin(lengths, slabs, own, rows)
    pieces = gather_four(own, top) if blocks == 4 else gather_row(own, blocks)
    top, acc = suffix_call([0], lengths, qm, top, acc, near)
    halo = [exchange(cut(r)) for r in raw]
    if blocks == 4:
        two, where = pieces[-1]
        two, top, _ = lax.optimization_barrier((two, top, [h[2:] for h in halo]))
        pieces = pieces[:-1] + [(two, where), pass_on(two)]
    for back in range(1, reach + 1):
        top, acc = suffix_call([back], lengths, qm, top, acc, halo[back - 1])
    top, acc = prefix_call(lengths, qm, top, acc, pieces[:3])
    far = finish(1, lengths, qm, top, acc, pieces[3:])
    near = finish(0, lengths, qm, top, acc, pieces[3:])
    return join(exchange([*near, *far]))


def solution(mesh):
    in_specs = (
        P("grp", "req", None),
        P("grp", None, "req", None),
        P("grp", None, "req", None),
        P("grp", None),
    )
    out_specs = P("grp", "req", None)
    return jax.shard_map(
        on_device, mesh=mesh, in_specs=in_specs, out_specs=out_specs, check_vma=False
    )
```
